256 devices in a mesh: dp: 32 (over x, z), expert: 8 (over y, core).
Axes of the slice: x: 4, y: 4, z: 8, core: 2. Of those that a mesh axis runs over, the one named last changes fastest.
Arguments:
- tokens: bfloat16 [4096, 4096], P('dp', 'expert'), may hold values from -6 to 6
- cotangent: bfloat16 [4096, 4096], P('dp', 'expert'), may hold values from -6 to 6
- expert_ids: int32 [4096, 8], P('dp'), may hold values from 0 to 63, all different within a row; in each aligned block of 128 rows (0 to 127, 128 to 255, ...) at most 24 rows name the same one
- gate_values: float32 [4096, 8], P('dp'), may hold values from 0.05 to 0.5
- swap_plan: int32 [32], replicated, may hold values from 0 to 1, as said below
- gate_weight: bfloat16 [64, 4096, 768], P('dp', 'expert'), may hold values from -0.09375 to 0.09375
- up_weight: bfloat16 [64, 4096, 768], P('dp', 'expert'), may hold values from -0.09375 to 0.09375
- down_weight: bfloat16 [64, 768, 4096], P('dp', None, 'expert'), may hold values from -0.21875 to 0.21875
Outputs:
- token_grad: bfloat16 [4096, 4096], P('dp', 'expert')
- gate_grad: bfloat16 [64, 4096, 768], P('dp', 'expert')
- up_grad: bfloat16 [64, 4096, 768], P('dp', 'expert')
- down_grad: bfloat16 [64, 768, 4096], P('dp', None, 'expert')
The draws below stay inside these ranges and needn't reach their ends.
Inputs may be any that keep to these rules, and one draw needn't show every extreme that they name: `expert_ids`: in each aligned block of 128 rows (the tokens of one dp index) no expert is named by more than 24 rows; the 8 experts of a row are distinct. swap_plan[p] equals swap_plan[p + 16] for p < 16.
All inputs are finite; a program needn't handle non-finite values.
Results may differ from the reference program's by a relative error of at most 0.0058.
Values may be sent and summed in bfloat16 or wider, within the bound.
A program may use at most 128 MiB of HBM per device.

```python
import math
import jax
import jax.numpy as jnp
import numpy as np
from jax import lax

D = 4096
FF = 768
TOP = 8
EXP_DP = 2
TOK = 128
EXPERTS = 64
TOKENS = 4096
MOST = 24
HALF = 16
N_DP = 32


def draw_swap_plan(key, part):
    key = jax.random.fold_in(key, 7)
    flags = jax.random.randint(key, (HALF,), 0, 2).astype(jnp.int32)
    flags = flags.at[0].set(1).at[HALF - 1].set(1)
    return jnp.concatenate([flags, flags])


def shard_levels(own_key, shape, shards, low, largest):
    def one(axis_at, blocks):
        draws = jax.random.uniform(jax.random.fold_in(jax.random.fold_in(own_key, 6), axis_at), (blocks,), jnp.float32, low / len(shards), largest / len(shards))
        return jnp.repeat(jnp.exp(draws), shape[axis_at] // blocks).reshape((-1,) + (1,) * (len(shape) - axis_at - 1))

    level = one(*shards[0])
    for cut in shards[1:]:
        level = level * one(*cut)
    return level


def deal_out(rng, own, number, rows, count, top, bound, slope):
    ranking = jax.random.permutation(rng, count)
    heavy_load, usual = load_shares(count, rows * top, bound, slope, True), load_shares(count, rows * top, bound, slope, False)
    places = jnp.arange(count)

    def named(lengths, rotation):
        used = int((lengths > 0).sum())
        fixed = max(1, used // 4)
        shifted = fixed + (places - fixed + rotation * (used - fixed)) % max(1, count - fixed)
        return jnp.zeros((count,), jnp.int32).at[ranking[jnp.where(places < fixed, places, shifted)]].set(jnp.asarray(lengths, jnp.int32))

    lengths = jnp.where(number % 4 == 0, named(heavy_load, number // 4), named(usual, number - number // 4 - 1))
    mixed = jax.random.permutation(jax.random.fold_in(own, 3), count)
    source_of, sink = mixed[0:count // 2 * 2:2], mixed[1:count // 2 * 2:2]
    slack = jnp.minimum(lengths[source_of] - 1, bound - lengths[sink]) // 2
    slack = jnp.where((source_of == ranking[0]) | (sink == ranking[0]) | (lengths[sink] == 0), 0, jnp.maximum(slack, 0))
    shifted = jax.random.randint(jax.random.fold_in(own, 4), (count // 2,), 0, 1 << 20) % (slack + 1)
    lengths = lengths.at[source_of].add(-shifted).at[sink].add(shifted)
    items = jnp.searchsorted(jnp.cumsum(lengths), jnp.arange(rows * top), side="right").astype(jnp.int32)
    grid = items.reshape(top, rows).T
    grid = grid[jax.random.permutation(jax.random.fold_in(own, 1), rows)]
    rotation = jax.random.randint(jax.random.fold_in(own, 2), (rows, 1), 0, top)
    return jnp.take_along_axis(grid, (jnp.arange(top)[None, :] + rotation) % top, axis=1)


def load_shares(number_of, total, limit, lean, full):
    portions = [(1 << 20) // math.isqrt(grade ** lean) + 1 for grade in range(1, number_of + 1)]
    largest = limit if full else min(limit, max(-(-total // number_of), total * portions[0] // sum(portions)))
    least = 1 if total - largest >= number_of - 1 else 0
    given, spare = [largest] + [least] * (number_of - 1), total - largest - least * (number_of - 1)
    while spare > 0:
        candidates = [i for i in range(1, number_of) if given[i] < largest] or [i for i in range(1, number_of) if given[i] < limit]
        mass, remaining = sum([portions[i] for i in candidates]), spare
        for i in candidates:
            addition = min(limit - given[i], max(1, remaining * portions[i] // mass), spare)
            given[i] = given[i] + addition
            spare = spare - addition
    return np.array(given)


def scatter_about(own_key, shape, scale, most, split=(), kind=jnp.bfloat16):
    array = scale * jax.random.normal(own_key, shape, jnp.float32)
    if split:
        array = array * shard_levels(own_key, shape, split, -0.22, 0.18)
    return jnp.clip(array, -most, most).astype(kind)


def setup_inputs(seed: int = 0) -> dict:
    arg_keys = jax.random.split(jax.random.key(seed), 9)
    tokens = scatter_about(arg_keys[0], (TOKENS, D), 1.0, 6.0, ((0, 32), (1, 8)))
    cotangent = scatter_about(arg_keys[1], (TOKENS, D), 1.0, 6.0, ((0, 32), (1, 8)))
    expert_ids_keys = jax.random.split(jax.random.fold_in(arg_keys[2], 1), TOKENS // TOK)
    expert_ids_turns = jax.random.permutation(jax.random.fold_in(arg_keys[2], 3), TOKENS // TOK)
    expert_ids = jax.vmap(lambda own, number: deal_out(jax.random.fold_in(arg_keys[2], 2), own, number, TOK, EXPERTS, TOP, MOST, 2))(expert_ids_keys, expert_ids_turns).reshape((TOKENS, TOP))
    gate_values = jnp.clip(jnp.exp(math.log(0.5) - 2.3025851 * jax.random.uniform(arg_keys[3], (TOKENS, TOP), jnp.float32) ** shard_levels(arg_keys[3], (TOKENS, TOP), ((0, 32),), -0.2, 0.2)), 0.05, 0.5)
    swap_plan = draw_swap_plan(jax.random.fold_in(arg_keys[8], 71), 0)
    gate_weight = scatter_about(arg_keys[5], (EXPERTS, D, FF), D ** -0.5, 0.09375, ((0, 32), (1, 8)))
    up_weight = scatter_about(arg_keys[6], (EXPERTS, D, FF), D ** -0.5, 0.09375, ((0, 32), (1, 8)))
    down_weight = scatter_about(arg_keys[7], (EXPERTS, FF, D), FF ** -0.5, 0.21875, ((0, 32), (2, 8)))
    return {"tokens": tokens, "cotangent": cotangent, "expert_ids": expert_ids, "gate_values": gate_values, "swap_plan": swap_plan, "gate_weight": gate_weight, "up_weight": up_weight, "down_weight": down_weight}


def reference(tokens, cotangent, expert_ids, gate_values, swap_plan, gate_weight, up_weight, down_weight):
    capacity = N_DP * MOST

    def per_expert(carry, expert):
        match = expert_ids == expert
        weight_sel = jnp.sum(jnp.where(match, gate_values, jnp.float32(0.0)), axis=1)
        chosen = jnp.any(match, axis=1)
        index = jnp.nonzero(chosen, size=capacity, fill_value=0)[0].astype(jnp.int32)
        valid = (jnp.arange(capacity, dtype=jnp.int32) < jnp.sum(chosen.astype(jnp.int32)))[:, None]
        rows = jnp.where(valid, tokens[index], jnp.zeros((), jnp.bfloat16))
        routed = (jnp.where(valid, weight_sel[index][:, None], jnp.float32(0.0)) * cotangent[index].astype(jnp.float32)).astype(jnp.bfloat16)
        w_gate = gate_weight[expert]
        w_up = up_weight[expert]
        w_down = down_weight[expert]
        gate_pre = jnp.dot(rows, w_gate, preferred_element_type=jnp.float32)
        up_pre = jnp.dot(rows, w_up, preferred_element_type=jnp.float32)
        back = jnp.dot(routed, w_down.T, preferred_element_type=jnp.float32)
        sig = jax.nn.sigmoid(gate_pre)
        silu = gate_pre * sig
        hidden = (silu * up_pre).astype(jnp.bfloat16)
        gate_delta = (back * up_pre * sig * (1.0 + gate_pre * (1.0 - sig))).astype(jnp.bfloat16)
        up_delta = (back * silu).astype(jnp.bfloat16)
        gate_sum = jnp.dot(rows.T, gate_delta, preferred_element_type=jnp.float32)
        up_sum = jnp.dot(rows.T, up_delta, preferred_element_type=jnp.float32)
        down_sum = jnp.dot(hidden.T, routed, preferred_element_type=jnp.float32)
        token_part = jnp.dot(gate_delta, w_gate.T, preferred_element_type=jnp.float32) + jnp.dot(up_delta, w_up.T, preferred_element_type=jnp.float32)
        token_part = jnp.where(valid, token_part, jnp.float32(0.0))
        carry = carry.at[index].add(token_part)
        return carry, (gate_sum.astype(jnp.bfloat16), up_sum.astype(jnp.bfloat16), down_sum.astype(jnp.bfloat16))

    start = jnp.zeros((TOKENS, D), jnp.float32)
    total, (gate_all, up_all, down_all) = lax.scan(per_expert, start, jnp.arange(EXPERTS, dtype=jnp.int32))
    slots = jnp.arange(EXPERTS, dtype=jnp.int32)
    host = slots // EXP_DP
    inner = slots % EXP_DP
    moved = (inner == EXP_DP - 1) & (swap_plan[host] == 1)
    holder = jnp.where(moved, ((host + HALF) % (2 * HALF)) * EXP_DP + inner, slots)
    return total.astype(jnp.bfloat16), gate_all[holder], up_all[holder], down_all[holder]
```

```python
import functools

import jax
import jax.numpy as jnp
from jax import lax
from jax.experimental import pallas as pl
from jax.experimental.pallas import tpu as pltpu
from jax.sharding import PartitionSpec as P

BF = jnp.bfloat16
F32 = jnp.float32
MESH = pl.DeviceIdType.MESH
NX, NZ, NY = 4, 8, 4
FF = 768


def dot(a, b):
    return lax.dot_general(a, b, (((1,), (0,)), ((), ())), preferred_element_type=F32)


def dot_nt(a, b):
    return lax.dot_general(a, b, (((1,), (1,)), ((), ())), preferred_element_type=F32)


def dot_tn(a, b):
    return lax.dot_general(a, b, (((0,), (0,)), ((), ())), preferred_element_type=F32)


def kernel(
    plan, tok, cot, meta, wg, wu, wd,
    tg_o, gg_o, ug_o, dg_o,
    T, C, M, X, G, RK, GV, RK2, CS, CR, H, SY, RY, PS, PR, AB0, ABA, ABB, R, RB, DS, ZR,
    ax_s, ax_r, az_s, az_r, bz_s, bz_r, bx_s, bx_r, cs_s, cs_r, sy_s, sy_r,
    ps_s, ps_r, ag_s, ag_r, rx_s, rx_r, rz_s, rz_r,
):
    dp = lax.axis_index("dp")
    ex = lax.axis_index("expert")
    x, z = lax.div(dp, NZ), lax.rem(dp, NZ)
    y, c = lax.div(ex, 2), lax.rem(ex, 2)

    def at(xx, zz):
        return lax.rem(xx, NX) * NZ + lax.rem(zz, NZ)

    def yc(yy, cc):
        return lax.rem(yy, NY) * 2 + cc

    peer = (dp, yc(y, 1 - c))
    up_y, down_y = (dp, yc(y + 1, c)), (dp, yc(y + 3, c))
    x_to = [None] + [(at(x + j, z), ex) for j in (1, 2, 3)]
    z_to = [None] + [(at(x, z + i), ex) for i in range(1, NZ)]

    barrier = pltpu.get_barrier_semaphore()
    others = [peer, up_y, down_y] + x_to[1:] + z_to[1:]
    for other in others:
        pl.semaphore_signal(barrier, inc=1, device_id=other, device_id_type=MESH)
    pl.semaphore_wait(barrier, len(others))

    sent = []

    def go(src, dst, s, r, to):
        copy = pltpu.make_async_remote_copy(
            src_ref=src, dst_ref=dst, send_sem=s, recv_sem=r, device_id=to, device_id_type=MESH
        )
        copy.start()
        sent.append(copy)
        return copy

    ax, az, bz, bx = {}, {}, {}, {}

    def send_az(way, j, h):
        for a, buf in enumerate((T, M)):
            b = at(x + 4 - j, z + (8 - (h - 1) if way == 0 else h - 1))
            src = buf.at[b] if (j or h > 1) else (tok, meta)[a]
            az[way, a, j, h] = go(
                src, buf.at[b], az_s.at[way, a, j, h - 1], az_r.at[way, a, j, h - 1],
                z_to[1] if way == 0 else z_to[7],
            )

    def send_bz(way, h):
        b = at(x, z + (8 - (h - 1) if way == 0 else h - 1))
        src = C.at[b] if h > 1 else cot
        bz[way, h] = go(
            src, C.at[b], bz_s.at[way, h - 1], bz_r.at[way, h - 1], z_to[1] if way == 0 else z_to[7]
        )

    def send_bx(d):
        b = at(x, z + d)
        for j in (1, 2, 3):
            bx[j, d] = go(
                C.at[b] if d else cot, C.at[b], bx_s.at[j - 1, d], bx_r.at[j - 1, d], x_to[j]
            )

    for j in (1, 2, 3):
        for a, (buf, src) in enumerate(((T, tok), (M, meta))):
            ax[a, j] = go(src, buf.at[dp], ax_s.at[a, j - 1], ax_r.at[a, j - 1], x_to[j])
    send_bz(0, 1)
    send_bz(1, 1)
    send_az(0, 0, 1)
    send_az(1, 0, 1)
    send_bx(0)
    T[dp] = tok[...]
    C[dp] = cot[...]
    M[dp] = meta[...]
    last = lambda way, j: 4 if (j + way) % 2 == 0 else 3
    for j in (1, 2, 3):
        for a in (0, 1):
            ax[a, j].wait_recv()
        send_az(0, j, 1)
        send_az(1, j, 1)
    for h in (1, 2, 3, 4):
        for way in (0, 1):
            if h <= 4 - way:
                bz[way, h].wait_recv()
                if h < 4 - way:
                    send_bz(way, h + 1)
                send_bx(8 - h if way == 0 else h)
        for j in range(4):
            for way in (0, 1):
                if h <= last(way, j):
                    for a in (0, 1):
                        az[way, a, j, h].wait_recv()
                    if h < last(way, j):
                        send_az(way, j, h + 1)

    flag = jnp.full((1, 128), plan[dp].astype(F32))
    far = lax.rem(dp + NX * NZ // 2, NX * NZ)
    own_id = (2 * dp + 1).astype(F32)
    star_id = flag * (2 * far + 1).astype(F32) + (1.0 - flag) * own_id
    row_i = lax.broadcasted_iota(jnp.int32, (128, 128), 0)
    col_i = lax.broadcasted_iota(jnp.int32, (128, 128), 1)
    upper = jnp.where(row_i <= col_i, 1.0, 0.0).astype(BF)

    def places(ids, target):
        match = ids == target
        hit = jnp.sum(jnp.where(match, 1.0, 0.0), axis=1)
        return match, jnp.where(hit > 0.0, dot(hit.astype(BF), upper) - 1.0, -1000.0)

    ids, gates = M[:, 0:8, :], M[:, 8:16, :]
    for i, target in enumerate(((2 * dp).astype(F32), own_id, star_id[:, None, :])):
        match, rank = places(ids, target)
        RK[i] = rank
        GV[i] = jnp.sum(jnp.where(match, gates, 0.0), axis=1)
    near = M[pl.ds(pl.multiple_of(x * NZ, NZ), NZ), 0:8, :]
    for e in (0, 1):
        for j in range(4):
            _, rank = places(near, (2 * at(x + 4 - j, z) + e).astype(F32))
            RK2[e * 4 + j] = rank

    for j in (1, 2, 3):
        for d in range(8):
            bx[j, d].wait_recv()

    slot_i = lax.broadcasted_iota(jnp.int32, (48, 256), 0).astype(F32)

    def pick(q, carry):
        ones, scale = [], []
        for i in range(3):
            r0 = RK[i, pl.ds(2 * q, 1), :]
            r1 = RK[i, pl.ds(2 * q + 1, 1), :] + 24.0
            eq = slot_i == jnp.concatenate([r0, r1], axis=1)
            g = jnp.concatenate([GV[i, pl.ds(2 * q, 1), :], GV[i, pl.ds(2 * q + 1, 1), :]], axis=1)
            ones.append(jnp.where(eq, 1.0, 0.0).astype(BF))
            scale.append(jnp.sum(jnp.where(eq, g, 0.0), axis=1, keepdims=True))
        ones = jnp.concatenate(ones, axis=0)
        scale = jnp.concatenate(scale, axis=0)
        xs = dot(ones, T[pl.ds(2 * q, 2)].reshape(256, 512)).astype(BF)
        gs = (dot(ones, C[pl.ds(2 * q, 2)].reshape(256, 512)) * scale).astype(BF)
        at_row = pl.ds(pl.multiple_of(48 * q, 16), 48)
        for i in range(3):
            X[i, at_row, :] = xs[48 * i : 48 * i + 48]
            G[i, at_row, :] = gs[48 * i : 48 * i + 48]
        return carry

    lax.fori_loop(0, 16, pick, 0)

    cs = {}

    def project(e, mine):
        rows = pl.ds(pl.multiple_of((c if mine else 1 - c) * 384, 384), 384)
        xs, gs = X[e, rows, :], G[e, rows, :]
        for n in range(9):
            t = slice(n % 3 * 256, n % 3 * 256 + 256)
            if n < 3:
                res = dot(xs, wg[e, :, t])
            elif n < 6:
                res = dot(xs, wu[e, :, t])
            else:
                res = dot_nt(gs, wd[e, t, :])
            if mine:
                H[e, :, n * 256 : n * 256 + 256] = res
            else:
                CS[e, :, n * 256 : n * 256 + 256] = res.astype(BF)
        if not mine:
            cs[e] = go(CS.at[e], CR.at[e], cs_s.at[e], cs_r.at[e], peer)

    sy = {}

    def part(e, yy, off, col):
        rows = pl.ds(pl.multiple_of(lax.rem(yy, NY) * 96 + off, 16), 48)
        return H[e, rows, col] + CR[e, rows, col].astype(F32)

    def tiles(body, n=9, width=256):
        def step(i, carry):
            body(pl.ds(pl.multiple_of(i * width, width), width))
            return carry

        lax.fori_loop(0, n, step, 0)

    def message(e, m, yy, off, plus=None):
        def body(col):
            v = part(e, yy, off, col)
            if plus is not None:
                v = v + RY[e, plus, :, col].astype(F32)
            SY[e, m, :, col] = v.astype(BF)

        tiles(body)
        sy[e, m] = go(
            SY.at[e, m], RY.at[e, m], sy_s.at[e, m], sy_r.at[e, m], up_y if m in (0, 1, 4) else down_y
        )

    def ring_one(e):
        cs[e].wait_recv()
        message(e, 0, y + 2, 0)
        message(e, 2, y + 2, 48)
        message(e, 1, y + 1, 48)
        message(e, 3, y + 3, 0)

    def ring_two(e):
        sy[e, 0].wait_recv()
        message(e, 4, y + 1, 0, plus=0)
        sy[e, 2].wait_recv()
        message(e, 5, y + 3, 48, plus=2)

    mine = c * 4 + y

    def activate(e):
        for m in (1, 3, 4, 5):
            sy[e, m].wait_recv()
        for rr in (0, 1):
            rows = slice(rr * 48, rr * 48 + 48)
            a, b = ((4, 3), (5, 1))[rr]

            def body(i, carry):
                def total(kind):
                    col = pl.ds(pl.multiple_of(kind * FF + i * 128, 128), 128)
                    v = part(e, y, rr * 48, col)
                    return v + RY[e, a, :, col].astype(F32) + RY[e, b, :, col].astype(F32)

                gate, up, back = total(0), total(1), total(2)
                sig = jax.nn.sigmoid(gate)
                silu = gate * sig
                hid = (silu * up).astype(BF)
                gd = (back * up * sig * (1.0 + gate * (1.0 - sig))).astype(BF)
                ud = (back * silu).astype(BF)
                cols = [pl.ds(pl.multiple_of(k * FF + i * 128, 128), 128) for k in range(3)]
                if e == 0:
                    for k, v in enumerate((hid, gd, ud)):
                        AB0[mine, rows, cols[k]] = v
                else:
                    for k, v in enumerate((hid, gd, ud)):
                        PS[rows, cols[k]] = v
                    ABA[mine, rows, cols[0]] = gd
                    ABA[mine, rows, cols[1]] = ud
                return carry

            lax.fori_loop(0, 6, body, 0)

    ag = {}
    ABS = (ABA, ABB, AB0)

    def ag_own(i):
        own = ABS[i].at[mine]
        for n, to in ((0, up_y), (1, down_y), (2, peer)):
            ag[i, n] = go(own, own, ag_s.at[i, n], ag_r.at[i, n], to)

    def ag_pass(i):
        for n, (yy, off, to) in enumerate(((y + 3, 0, up_y), (y + 1, 48, down_y))):
            ag[i, n].wait_recv()
            k = c * 4 + lax.rem(yy, NY)
            part_ref = ABS[i].at[k, pl.ds(off, 48)]
            ag[i, 3 + n] = go(part_ref, part_ref, ag_s.at[i, 3 + n], ag_r.at[i, 3 + n], to)
            whole = ABS[i].at[k]
            ag[i, 5 + n] = go(whole, whole, ag_s.at[i, 5 + n], ag_r.at[i, 5 + n], peer)

    def ag_end(i):
        ag[i, 3].wait_recv()
        ag[i, 4].wait_recv()
        whole = ABS[i].at[c * 4 + lax.rem(y + 2, NY)]
        ag[i, 7] = go(whole, whole, ag_s.at[i, 7], ag_r.at[i, 7], peer)

    def ag_done(i):
        for n in (2, 5, 6, 7):
            ag[i, n].wait_recv()

    rx = {}

    def back_rows(e):
        ab, g0 = (AB0, FF) if e == 0 else (ABA, 0)

        def step(i, carry):
            k = pl.ds(pl.multiple_of(i * 4, 4), 4)
            gd = ab[k, :, g0 : g0 + FF].reshape(384, FF)
            ud = ab[k, :, g0 + FF : g0 + 2 * FF].reshape(384, FF)
            for n in (0, 256):
                res = dot_nt(gd, wg[e, n : n + 256, :]) + dot_nt(ud, wu[e, n : n + 256, :])
                R[e, pl.ds(pl.multiple_of(i * 8, 8), 8), :, n : n + 256] = res.astype(BF).reshape(8, 48, 256)
            return carry

        lax.fori_loop(0, 2, step, 0)
        for j in (1, 2, 3):
            q = pl.ds(pl.multiple_of(lax.rem(x + j, NX) * 4, 4), 4)
            rx[e, j] = go(
                R.at[e, q], RB.at[:, e * 4 + j], rx_s.at[e, j - 1], rx_r.at[e, j - 1], x_to[j]
            )
        RB[:, e * 4] = R[e, pl.ds(pl.multiple_of(x * 4, 4), 4)]

    def weight_grads(slot, ab, h0, i):
        def inputs(n, carry):
            d = pl.ds(pl.multiple_of(n * 256, 256), 256)
            xs = X[i, :, d]
            for k, out in ((1, gg_o), (2, ug_o)):
                act = ab[:, :, h0 + k * FF : h0 + (k + 1) * FF].reshape(FF, FF)
                out[slot, d, :] = dot_tn(xs, act).astype(BF)
            return carry

        lax.fori_loop(0, 2, inputs, 0)

        def hidden(n, carry):
            f = pl.ds(pl.multiple_of(n * 256, 256), 256)
            hid = ab[:, :, pl.ds(pl.multiple_of(h0 + n * 256, 256), 256)].reshape(FF, 256)
            dg_o[slot, f, :] = dot_tn(hid, G[i]).astype(BF)
            return carry

        lax.fori_loop(0, 3, hidden, 0)

    project(1, False)
    project(1, True)
    ring_one(1)
    project(0, False)
    project(0, True)
    ring_two(1)
    ring_one(0)
    activate(1)
    swap = go(PS, PR, ps_s.at[0], ps_r.at[0], x_to[2])
    ag_own(0)
    ring_two(0)
    ag_pass(0)
    swap.wait_recv()

    def choose(col):
        keep = jnp.full((96, 256), plan[dp].astype(F32)) > 0.5
        v = jnp.where(keep, PR[:, col].astype(F32), PS[:, col].astype(F32))
        ABB[mine, :, col] = v.astype(BF)

    tiles(choose)
    ag_own(1)
    activate(0)
    ag_own(2)
    ag_end(0)
    ag_pass(1)
    ag_done(0)
    back_rows(1)
    ag_end(1)
    ag_pass(2)
    ag_done(1)
    weight_grads(1, ABB, 0, 2)
    ag_end(2)
    ag_done(2)
    back_rows(0)

    for e in (1, 0):
        for j in (1, 2, 3):
            rx[e, j].wait_recv()

    def dense(p):
        pieces = []
        for s in range(8):
            r0 = RK2[s, pl.ds(2 * p, 1), :]
            r1 = RK2[s, pl.ds(2 * p + 1, 1), :] + 24.0
            pieces.append(
                jnp.where(slot_i == jnp.concatenate([r0, r1], axis=1), 1.0, 0.0).astype(BF)
            )
        return dot_tn(jnp.concatenate(pieces, axis=0), RB[p].reshape(384, 512))

    def rz_copy(zt):
        return pltpu.make_async_remote_copy(
            src_ref=DS.at[zt], dst_ref=ZR.at[z], send_sem=rz_s.at[zt], recv_sem=rz_r.at[z],
            device_id=(at(x, zt), ex), device_id_type=MESH,
        )

    half = lax.div(z, 2)

    def spread(i, carry):
        p = lax.rem(half + 1 + i, 4)
        v = dense(p)
        DS[pl.ds(2 * p, 2)] = v.astype(BF).reshape(2, 128, 512)
        rz_copy(2 * p).start()
        rz_copy(2 * p + 1).start()
        return carry

    lax.fori_loop(0, 3, spread, 0)
    v = dense(half)
    DS[pl.ds(2 * half, 2)] = v.astype(BF).reshape(2, 128, 512)
    mate = 2 * half + 1 - lax.rem(z, 2)
    rz_copy(mate).start()

    weight_grads(0, AB0, 0, 0)

    total = DS[z].astype(F32)
    for i in range(1, 8):
        zs = lax.rem(z + i, NZ)
        pltpu.make_async_remote_copy(
            src_ref=DS.at[zs], dst_ref=ZR.at[zs], send_sem=rz_s.at[zs], recv_sem=rz_r.at[zs],
            device_id=(at(x, zs), ex), device_id_type=MESH,
        ).wait()
        total = total + ZR[zs].astype(F32)
    tg_o[...] = total.astype(BF)
    for copy in sent:
        copy.wait_send()


def shards(tokens, cotangent, expert_ids, gate_values, swap_plan, gate_weight, up_weight, down_weight):
    meta = jnp.concatenate([expert_ids.T.astype(F32), gate_values.T], axis=0)
    vmem = pl.BlockSpec(memory_space=pltpu.VMEM)
    dma = lambda *shape: [pltpu.SemaphoreType.DMA(shape), pltpu.SemaphoreType.DMA(shape)]
    w = 3 * FF
    return pl.pallas_call(
        kernel,
        out_shape=(
            jax.ShapeDtypeStruct(tokens.shape, BF),
            jax.ShapeDtypeStruct(gate_weight.shape, BF),
            jax.ShapeDtypeStruct(up_weight.shape, BF),
            jax.ShapeDtypeStruct(down_weight.shape, BF),
        ),
        in_specs=[pl.BlockSpec(memory_space=pltpu.SMEM)] + [vmem] * 6,
        out_specs=(vmem,) * 4,
        scratch_shapes=[
            pltpu.VMEM((32, 128, 512), BF),
            pltpu.VMEM((32, 128, 512), BF),
            pltpu.VMEM((32, 16, 128), F32),
            pltpu.VMEM((3, 768, 512), BF),
            pltpu.VMEM((3, 768, 512), BF),
            pltpu.VMEM((3, 32, 128), F32),
            pltpu.VMEM((3, 32, 128), F32),
            pltpu.VMEM((8, 8, 128), F32),
            pltpu.VMEM((2, 384, w), BF),
            pltpu.VMEM((2, 384, w), BF),
            pltpu.VMEM((2, 384, w), F32),
            pltpu.VMEM((2, 6, 48, w), BF),
            pltpu.VMEM((2, 6, 48, w), BF),
            pltpu.VMEM((96, w), BF),
            pltpu.VMEM((96, w), BF),
            pltpu.VMEM((8, 96, w), BF),
            pltpu.VMEM((8, 96, 2 * FF), BF),
            pltpu.VMEM((8, 96, w), BF),
            pltpu.VMEM((2, 16, 48, 512), BF),
            pltpu.VMEM((4, 8, 48, 512), BF),
            pltpu.VMEM((8, 128, 512), BF),
            pltpu.VMEM((8, 128, 512), BF),
        ]
        + dma(2, 3)
        + dma(2, 2, 4, 4)
        + dma(2, 4)
        + dma(3, 8)
        + dma(2)
        + dma(2, 6)
        + dma(1)
        + dma(3, 8)
        + dma(2, 3)
        + dma(8),
        compiler_params=pltpu.CompilerParams(
            collective_id=0, has_side_effects=True, vmem_limit_bytes=62 << 20
        ),
        cost_estimate=pl.CostEstimate(flops=10_000_000_000, bytes_accessed=10_000_000, transcendentals=0),
        name="expert_layer",
    )(swap_plan, tokens, cotangent, meta, gate_weight, up_weight, down_weight)


def solution(mesh):
    return jax.shard_map(
        shards,
        mesh=mesh,
        in_specs=(
            P("dp", "expert"),
            P("dp", "expert"),
            P("dp", None),
            P("dp", None),
            P(),
            P("dp", "expert", None),
            P("dp", "expert", None),
            P("dp", None, "expert"),
        ),
        out_specs=(
            P("dp", "expert"),
            P("dp", "expert", None),
            P("dp", "expert", None),
            P("dp", None, "expert"),
        ),
        check_vma=False,
    )
```

```python
import functools

import jax
import jax.numpy as jnp
from jax import lax
from jax.experimental import pallas as pl
from jax.experimental.pallas import tpu as pltpu
from jax.sharding import PartitionSpec as P

BF = jnp.bfloat16
F32 = jnp.float32
MESH = pl.DeviceIdType.MESH
NX, NZ, NY = 4, 8, 4
FF = 768


def dot(a, b):
    return lax.dot_general(a, b, (((1,), (0,)), ((), ())), preferred_element_type=F32)


def dot_nt(a, b):
    return lax.dot_general(a, b, (((1,), (1,)), ((), ())), preferred_element_type=F32)


def dot_tn(a, b):
    return lax.dot_general(a, b, (((0,), (0,)), ((), ())), preferred_element_type=F32)


def kernel(
    plan, tok, cot, ids_in, gates_in, wg, wu, wd,
    tg_o, gg_o, ug_o, dg_o,
    T, C, M, X, G, RK, GV, RK2, CS, CR, H, SY, RY, PS, PR, AB, AH, R, RB, DS, ZR, OWN,
    mx_s, mx_r, mz_s, mz_r, ax_s, ax_r, az_s, az_r, bz_s, bz_r, bx_s, bx_r, cs_s, cs_r,
    sy_s, sy_r, ps_s, ps_r, ag_s, ag_r, ah_s, ah_r, rx_s, rx_r, rz_s, rz_r,
):
    dp = lax.axis_index("dp")
    ex = lax.axis_index("expert")
    x, z = lax.div(dp, NZ), lax.rem(dp, NZ)
    y, c = lax.div(ex, 2), lax.rem(ex, 2)
    other = 1 - c

    def at(xx, zz):
        return lax.rem(xx, NX) * NZ + lax.rem(zz, NZ)

    turn = 1 + 2 * c
    y_a, y_b, y_opp = lax.rem(y + turn, NY), lax.rem(y + NY - turn, NY), lax.rem(y + 2, NY)
    peer = (dp, y * 2 + other)
    to_a, to_b = (dp, y_a * 2 + c), (dp, y_b * 2 + c)
    x_to = [None] + [(at(x + j, z), ex) for j in (1, 2, 3)]
    z_to = [None] + [(at(x, z + i), ex) for i in range(1, NZ)]

    barrier = pltpu.get_barrier_semaphore()
    group = [peer, to_a, to_b] + x_to[1:] + z_to[1:]
    for device in group:
        pl.semaphore_signal(barrier, inc=1, device_id=device, device_id_type=MESH)
    pl.semaphore_wait(barrier, len(group))

    def rc(src, dst, s, r, to):
        return pltpu.make_async_remote_copy(
            src_ref=src, dst_ref=dst, send_sem=s, recv_sem=r, device_id=to, device_id_type=MESH
        )

    sent = []

    def go(*how):
        copy = rc(*how)
        copy.start()
        sent.append(copy)
        return copy

    mx, mz, ax, az, bz, bx = {}, {}, {}, {}, {}, {}

    def send_az(way, j, h):
        b = at(x + 4 - j, z + (8 - (h - 1) if way == 0 else h - 1))
        az[way, j, h] = go(
            T.at[b] if (j or h > 1) else tok, T.at[b], az_s.at[way, j, h - 1], az_r.at[way, j, h - 1],
            z_to[1] if way == 0 else z_to[7],
        )

    def send_bz(way, h):
        b = at(x, z + (8 - (h - 1) if way == 0 else h - 1))
        bz[way, h] = go(
            C.at[b] if h > 1 else cot, C.at[b], bz_s.at[way, h - 1], bz_r.at[way, h - 1],
            z_to[1] if way == 0 else z_to[7],
        )

    def send_bx(d):
        b = at(x, z + d)
        for j in (1, 2, 3):
            bx[j, d] = go(
                C.at[b] if d else cot, C.at[b], bx_s.at[j - 1, d], bx_r.at[j - 1, d], x_to[j]
            )

    def last(way, j):
        return 4 if (j + way) % 2 == 0 else 3

    M[z, x, 0:8, :] = ids_in[...].astype(F32)
    M[z, x, 8:16, :] = gates_in[...]
    for j in (1, 2, 3):
        mx[j] = go(M.at[z, x], M.at[z, x], mx_s.at[j - 1], mx_r.at[j - 1], x_to[j])
    for j in (1, 2, 3):
        ax[j] = go(tok, T.at[dp], ax_s.at[j - 1], ax_r.at[j - 1], x_to[j])
    send_bz(0, 1)
    send_bz(1, 1)
    send_bx(0)
    for j in (1, 2, 3):
        mx[j].wait_recv()
    for i in range(1, NZ):
        mz[i] = go(M.at[z], M.at[z], mz_s.at[i], mz_r.at[i], z_to[i])
    send_az(0, 0, 1)
    send_az(1, 0, 1)
    T[dp] = tok[...]
    C[dp] = cot[...]
    for j in (1, 2, 3):
        ax[j].wait_recv()
        send_az(0, j, 1)
        send_az(1, j, 1)

    def hop(h):
        for way in (0, 1):
            if h <= 4 - way:
                bz[way, h].wait_recv()
                if h < 4 - way:
                    send_bz(way, h + 1)
                send_bx(8 - h if way == 0 else h)
        for j in range(4):
            for way in (0, 1):
                if h <= last(way, j):
                    az[way, j, h].wait_recv()
                    if h < last(way, j):
                        send_az(way, j, h + 1)

    def all_places():
        for i in range(1, NZ):
            mz[i].wait_recv()
        flag = jnp.full((1, 128), plan[dp].astype(F32))
        far = lax.rem(dp + NX * NZ // 2, NX * NZ)
        own_id = (2 * dp + 1).astype(F32)
        star_id = flag * (2 * far + 1).astype(F32) + (1.0 - flag) * own_id
        row_i = lax.broadcasted_iota(jnp.int32, (128, 128), 0)
        col_i = lax.broadcasted_iota(jnp.int32, (128, 128), 1)
        upper = jnp.where(row_i <= col_i, 1.0, 0.0).astype(BF)

        def places(ids, target):
            match = ids == target
            hit = jnp.sum(jnp.where(match, 1.0, 0.0), axis=1)
            return match, jnp.where(hit > 0.0, dot(hit.astype(BF), upper) - 1.0, -1000.0)

        ids = M[:, :, 0:8, :].reshape(32, 8, 128)
        gates = M[:, :, 8:16, :].reshape(32, 8, 128)
        for i, target in enumerate(((2 * dp).astype(F32), own_id, star_id[:, None, :])):
            match, rank = places(ids, target)
            RK[i] = rank
            GV[i] = jnp.sum(jnp.where(match, gates, 0.0), axis=1)
        near = M[:, pl.ds(x, 1), 0:8, :].reshape(8, 8, 128)
        for j in range(4):
            for e in (0, 1):
                _, rank = places(near, (2 * at(x + 4 - j, z) + e).astype(F32))
                RK2[j * 2 + e] = rank

    slot_i = lax.broadcasted_iota(jnp.int32, (48, 256), 0).astype(F32)

    def tiles(body, n=9, width=256):
        def step(i, carry):
            body(pl.ds(pl.multiple_of(i * width, width), width))
            return carry

        lax.fori_loop(0, n, step, 0)

    def pick(ch):
        for d in {(8 - ch) % 8, ch + 1}:
            for j in (1, 2, 3):
                bx[j, d].wait_recv()

        def step(j, carry):
            ba, bb = at(j, z + 8 - ch), at(j, z + 1 + ch)
            ra = lax.rem(z + 8 - ch, NZ) * 4 + j
            rb = lax.rem(z + 1 + ch, NZ) * 4 + j
            ones, scale = [], []
            for i in range(3):
                r0 = RK[i, pl.ds(ra, 1), :]
                r1 = RK[i, pl.ds(rb, 1), :] + 24.0
                eq = slot_i == jnp.concatenate([r0, r1], axis=1)
                g = jnp.concatenate([GV[i, pl.ds(ra, 1), :], GV[i, pl.ds(rb, 1), :]], axis=1)
                ones.append(jnp.where(eq, 1.0, 0.0).astype(BF))
                scale.append(jnp.sum(jnp.where(eq, g, 0.0), axis=1, keepdims=True))
            ones = jnp.concatenate(ones, axis=0)
            scale = jnp.concatenate(scale, axis=0)
            xs = dot(ones, jnp.concatenate([T[ba], T[bb]], axis=0)).astype(BF)
            gs = (dot(ones, jnp.concatenate([C[ba], C[bb]], axis=0)) * scale).astype(BF)
            rows = pl.ds(pl.multiple_of(48 * j, 16), 48)
            for i in range(3):
                X[i, ch, rows, :] = xs[48 * i : 48 * i + 48]
                G[i, ch, rows, :] = gs[48 * i : 48 * i + 48]
            return carry

        lax.fori_loop(0, 4, step, 0)

    cs, sy = {}, {}

    def project(ch):
        for own in (False, True):
            e = c if own else other
            for kind, w in enumerate((wg, wu, wd)):
                for n in range(0, FF, 256):
                    if kind < 2:
                        res = dot(X[e, ch], w[e, :, n : n + 256])
                    else:
                        res = dot_nt(G[e, ch], w[e, n : n + 256, :])
                    col = slice(kind * FF + n, kind * FF + n + 256)
                    if own:
                        H[ch % 2, :, col] = res
                    else:
                        CS[ch, :, col] = res.astype(BF)
            if not own:
                cs[ch] = go(CS.at[ch], CR.at[ch], cs_s.at[ch], cs_r.at[ch], peer)

    def part(ch, yy, col):
        rows = pl.ds(pl.multiple_of(yy * 48, 16), 48)
        return H[ch % 2, rows, col] + CR[ch, rows, col].astype(F32)

    def message(ch, m, yy, to, plus=None):
        def body(col):
            v = part(ch, yy, col)
            if plus is not None:
                v = v + RY[ch, plus, :, col].astype(F32)
            SY[ch, m, :, col] = v.astype(BF)

        tiles(body)
        sy[ch, m] = go(SY.at[ch, m], RY.at[ch, m], sy_s.at[ch, m], sy_r.at[ch, m], to)

    def ring_one(ch):
        cs[ch].wait_recv()
        message(ch, 0, y_opp, to_a)
        message(ch, 1, y_b, to_b)

    def ring_two(ch):
        sy[ch, 0].wait_recv()
        message(ch, 2, y_a, to_a, plus=0)

    swaps = lambda ch: rc(PS.at[ch], PR.at[ch], ps_s.at[ch], ps_r.at[ch], x_to[2])

    def activate(ch):
        sy[ch, 1].wait_recv()
        sy[ch, 2].wait_recv()

        def body(i, carry):
            cols = [pl.ds(pl.multiple_of(k * FF + i * 128, 128), 128) for k in range(3)]

            def total(col):
                v = part(ch, y, col)
                return v + RY[ch, 1, :, col].astype(F32) + RY[ch, 2, :, col].astype(F32)

            gate, up, back = [total(col) for col in cols]
            sig = jax.nn.sigmoid(gate)
            silu = gate * sig
            PS[ch, :, cols[0]] = (silu * up).astype(BF)
            PS[ch, :, cols[1]] = (back * up * sig * (1.0 + gate * (1.0 - sig))).astype(BF)
            PS[ch, :, cols[2]] = (back * silu).astype(BF)
            return carry

        lax.fori_loop(0, 6, body, 0)

        @pl.when(c == 1)
        def _():
            swaps(ch).start()
            AH[ch, y] = PS[ch, :, FF:]
            for n, to in ((0, to_a), (1, to_b), (2, peer)):
                ah(ch, n, y, to).start()

        @pl.when(c == 0)
        def _():
            AB[0, ch, y] = PS[ch]
            for n, to in ((0, to_a), (1, to_b), (2, peer)):
                ag(ch, n, y, to).start()

    def ag(ch, n, yy, to):
        block = AB.at[c, ch, yy]
        return rc(block, block, ag_s.at[ch, n], ag_r.at[ch, n], to)

    def ah(ch, n, yy, to):
        block = AH.at[ch, yy]
        return rc(block, block, ah_s.at[ch, n], ah_r.at[ch, n], to)

    def ag_in(ch, n):
        block = AB.at[other if n in (2, 4, 5, 6) else c, ch, y]
        return rc(block, block, ag_s.at[ch, n], ag_r.at[ch, n], peer)

    def choose(ch):
        @pl.when(c == 1)
        def _():
            swaps(ch).wait_recv()

            def body(col):
                keep = jnp.full((48, 256), plan[dp].astype(F32)) > 0.5
                v = jnp.where(keep, PR[ch, :, col].astype(F32), PS[ch, :, col].astype(F32))
                AB[1, ch, y, :, col] = v.astype(BF)

            tiles(body)
            for n, to in ((0, to_a), (1, to_b), (2, peer)):
                ag(ch, n, y, to).start()

    def ag_pass(ch):
        @pl.when(c == 1)
        def _():
            ah(ch, 0, y_b, to_a).wait_recv()
            ah(ch, 3, y_b, to_a).start()
            ah(ch, 4, y_b, peer).start()
            ah(ch, 1, y_a, to_b).wait_recv()
            ah(ch, 5, y_a, peer).start()

        ag_in(ch, 0).wait_recv()
        ag(ch, 3, y_b, to_a).start()
        ag(ch, 4, y_b, peer).start()
        ag_in(ch, 1).wait_recv()
        ag(ch, 5, y_a, peer).start()

    def ag_end(ch):
        @pl.when(c == 1)
        def _():
            ah(ch, 3, y_opp, to_a).wait_recv()
            ah(ch, 6, y_opp, peer).start()

        ag_in(ch, 3).wait_recv()
        ag(ch, 6, y_opp, peer).start()

    def ag_done(ch):
        @pl.when(c == 0)
        def _():
            for n in (2, 4, 5, 6):
                ah(ch, n, y, peer).wait_recv()

        for n in (2, 4, 5, 6):
            ag_in(ch, n).wait_recv()

    rx = {}

    def back_rows(ch):
        for e in (0, 1):
            gd = (AB[0, ch, :, :, FF : 2 * FF] if e == 0 else AH[ch, :, :, :FF]).reshape(192, FF)
            ud = (AB[0, ch, :, :, 2 * FF :] if e == 0 else AH[ch, :, :, FF:]).reshape(192, FF)
            for n in (0, 256):
                res = dot_nt(gd, wg[e, n : n + 256, :]) + dot_nt(ud, wu[e, n : n + 256, :])
                R[ch, e, :, :, n : n + 256] = res.astype(BF).reshape(4, 48, 256)
        for j in (1, 2, 3):
            rx[ch, j] = go(R.at[ch, :, lax.rem(x + j, NX)], RB.at[ch, j], rx_s.at[ch, j - 1], rx_r.at[ch, j - 1], x_to[j])

    rz = {}

    def spread(ch):
        for j in (1, 2, 3):
            rx[ch, j].wait_recv()
        za, zb = lax.rem(z + 8 - ch, NZ), lax.rem(z + 1 + ch, NZ)
        pieces = []
        for s in range(8):
            r0 = RK2[s, pl.ds(za, 1), :]
            r1 = RK2[s, pl.ds(zb, 1), :] + 24.0
            pieces.append(jnp.where(slot_i == jnp.concatenate([r0, r1], axis=1), 1.0, 0.0).astype(BF))
        own = dot_tn(jnp.concatenate(pieces[:2], axis=0), R[ch, :, pl.ds(x, 1)].reshape(96, 512))
        rest = dot_tn(jnp.concatenate(pieces[2:], axis=0), RB[ch, 1:].reshape(288, 512))
        v = own + rest
        for i, d in ((0, (8 - ch) % 8), (1, ch + 1)):
            block = v[128 * i : 128 * i + 128]
            if d == 0:
                OWN[...] = block
            else:
                DS[d] = block.astype(BF)
                rz[d] = go(DS.at[d], ZR.at[d], rz_s.at[d], rz_r.at[d], z_to[d])

    def input_grads(slot, i):
        def inputs(n, carry):
            d = pl.ds(pl.multiple_of(n * 256, 256), 256)
            xs = X[i, :, :, d].reshape(FF, 256)
            for k, out in ((1, gg_o), (2, ug_o)):
                act = AB[slot, :, :, :, k * FF : (k + 1) * FF].reshape(FF, FF)
                out[slot, d, :] = dot_tn(xs, act).astype(BF)
            return carry

        lax.fori_loop(0, 2, inputs, 0)

    def hidden_grads(slot, i):
        def hidden(n, carry):
            f = pl.ds(pl.multiple_of(n * 256, 256), 256)
            hid = AB[slot, :, :, :, f].reshape(FF, 256)
            dg_o[slot, f, :] = dot_tn(hid, G[i].reshape(FF, 512)).astype(BF)
            return carry

        lax.fori_loop(0, 3, hidden, 0)

    def forward(ch):
        pick(ch)
        project(ch)

    hop(1)
    all_places()
    forward(0)
    ring_one(0)
    hop(2)
    ring_two(0)
    forward(1)
    activate(0)
    ring_one(1)
    choose(0)
    hop(3)
    ring_two(1)
    ag_pass(0)
    forward(2)
    activate(1)
    ring_one(2)
    ag_end(0)
    choose(1)
    ring_two(2)
    ag_done(0)
    back_rows(0)
    ag_pass(1)
    hop(4)
    forward(3)
    activate(2)
    ring_one(3)
    ag_end(1)
    choose(2)
    spread(0)
    ring_two(3)
    ag_done(1)
    back_rows(1)
    ag_pass(2)
    activate(3)
    spread(1)
    ag_end(2)
    choose(3)
    ag_done(2)
    back_rows(2)
    ag_pass(3)
    spread(2)
    ag_end(3)
    ag_done(3)
    back_rows(3)
    hidden_grads(1, 2)
    spread(3)
    input_grads(1, 2)
    input_grads(0, 0)
    hidden_grads(0, 0)

    total = OWN[...]
    for d in (1, 7, 2, 6, 3, 5, 4):
        rz[d].wait_recv()
        total = total + ZR[d].astype(F32)
    tg_o[...] = total.astype(BF)
    for copy in sent:
        copy.wait_send()
    for ch in range(4):
        for n in range(7):
            ag(ch, n, y, peer).wait_send()

        @pl.when(c == 1)
        def _():
            swaps(ch).wait_send()
            for n in range(7):
                ah(ch, n, y, peer).wait_send()


def shards(tokens, cotangent, expert_ids, gate_values, swap_plan, gate_weight, up_weight, down_weight):
    vmem = pl.BlockSpec(memory_space=pltpu.VMEM)
    dma = lambda *shape: [pltpu.SemaphoreType.DMA(shape), pltpu.SemaphoreType.DMA(shape)]
    w = 3 * FF
    return pl.pallas_call(
        kernel,
        out_shape=(
            jax.ShapeDtypeStruct(tokens.shape, BF),
            jax.ShapeDtypeStruct(gate_weight.shape, BF),
            jax.ShapeDtypeStruct(up_weight.shape, BF),
            jax.ShapeDtypeStruct(down_weight.shape, BF),
        ),
        in_specs=[pl.BlockSpec(memory_space=pltpu.SMEM)] + [vmem] * 7,
        out_specs=(vmem,) * 4,
        scratch_shapes=[
            pltpu.VMEM((32, 128, 512), BF),
            pltpu.VMEM((32, 128, 512), BF),
            pltpu.VMEM((8, 4, 16, 128), F32),
            pltpu.VMEM((3, 4, 192, 512), BF),
            pltpu.VMEM((3, 4, 192, 512), BF),
            pltpu.VMEM((3, 32, 128), F32),
            pltpu.VMEM((3, 32, 128), F32),
            pltpu.VMEM((8, 8, 128), F32),
            pltpu.VMEM((4, 192, w), BF),
            pltpu.VMEM((4, 192, w), BF),
            pltpu.VMEM((2, 192, w), F32),
            pltpu.VMEM((4, 3, 48, w), BF),
            pltpu.VMEM((4, 3, 48, w), BF),
            pltpu.VMEM((4, 48, w), BF),
            pltpu.VMEM((4, 48, w), BF),
            pltpu.VMEM((2, 4, 4, 48, w), BF),
            pltpu.VMEM((4, 4, 48, 2 * FF), BF),
            pltpu.VMEM((4, 2, 4, 48, 512), BF),
            pltpu.VMEM((4, 4, 2, 48, 512), BF),
            pltpu.VMEM((8, 128, 512), BF),
            pltpu.VMEM((8, 128, 512), BF),
            pltpu.VMEM((128, 512), F32),
        ]
        + dma(3)
        + dma(8)
        + dma(3)
        + dma(2, 4, 4)
        + dma(2, 4)
        + dma(3, 8)
        + dma(4)
        + dma(4, 3)
        + dma(4)
        + dma(4, 7)
        + dma(4, 7)
        + dma(4, 3)
        + dma(8),
        compiler_params=pltpu.CompilerParams(
            collective_id=0, has_side_effects=True, vmem_limit_bytes=62 << 20
        ),
        cost_estimate=pl.CostEstimate(flops=10_000_000_000, bytes_accessed=10_000_000, transcendentals=0),
        name="expert_layer",
    )(
        swap_plan, tokens, cotangent, expert_ids.T, gate_values.T, gate_weight, up_weight, down_weight
    )


def solution(mesh):
    return jax.shard_map(
        shards,
        mesh=mesh,
        in_specs=(
            P("dp", "expert"),
            P("dp", "expert"),
            P("dp", None),
            P("dp", None),
            P(),
            P("dp", "expert", None),
            P("dp", "expert", None),
            P("dp", None, "expert"),
        ),
        out_specs=(
            P("dp", "expert"),
            P("dp", "expert", None),
            P("dp", "expert", None),
            P("dp", None, "expert"),
        ),
        check_vma=False,
    )
```

```python
import functools

import jax
import jax.numpy as jnp
from jax import lax
from jax.experimental import pallas as pl
from jax.experimental.pallas import tpu as pltpu
from jax.sharding import PartitionSpec as P

BF = jnp.bfloat16
F32 = jnp.float32
MESH = pl.DeviceIdType.MESH
NX, NZ, NY = 4, 8, 4
FF = 768


def dot(a, b):
    return lax.dot_general(a, b, (((1,), (0,)), ((), ())), preferred_element_type=F32)


def dot_nt(a, b):
    return lax.dot_general(a, b, (((1,), (1,)), ((), ())), preferred_element_type=F32)


def dot_tn(a, b):
    return lax.dot_general(a, b, (((0,), (0,)), ((), ())), preferred_element_type=F32)


def kernel(
    plan, tok, cot, ids_in, gates_in, wg_in, wu_in, wd_in,
    tg_out, gg_out, ug_out, dg_out,
    wg, wu, wd, tg_o, gg_o, ug_o, dg_o, near_s,
    T, C, M, M2, MF, X, G, RK, GV, RK2, CS, CR, H, SY, RY, PS, PR, AB, AH, R, RB, DS, ZR, OWN,
    mx_s, mx_r, mz_s, mz_r, ax_s, ax_r, az_s, az_r, bz_s, bz_r, bx_s, bx_r, cs_s, cs_r,
    sy_s, sy_r, ps_s, ps_r, ag_s, ag_r, ah_s, ah_r, rx_s, rx_r, rz_s, rz_r,
):
    dp = lax.axis_index("dp")
    ex = lax.axis_index("expert")
    x, z = lax.div(dp, NZ), lax.rem(dp, NZ)
    y, c = lax.div(ex, 2), lax.rem(ex, 2)
    other = 1 - c

    def at(xx, zz):
        return lax.rem(xx, NX) * NZ + lax.rem(zz, NZ)

    turn = 1 + 2 * c
    y_a, y_b, y_opp = lax.rem(y + turn, NY), lax.rem(y + NY - turn, NY), lax.rem(y + 2, NY)
    peer = (dp, y * 2 + other)
    to_a, to_b = (dp, y_a * 2 + c), (dp, y_b * 2 + c)
    x_to = [None] + [(at(x + j, z), ex) for j in (1, 2, 3)]
    z_to = [None] + [(at(x, z + i), ex) for i in range(1, NZ)]

    moves = [(wg_in, wg), (wu_in, wu), (wd_in, wd)]
    moves += [(gg_o.at[0], gg_out.at[0]), (ug_o.at[0], ug_out.at[0]), (dg_o.at[1], dg_out.at[1])]
    moves += [(gg_o.at[1], gg_out.at[1]), (ug_o.at[1], ug_out.at[1]), (dg_o.at[0], dg_out.at[0])]
    moves += [(tg_o, tg_out)]

    def local(n):
        return pltpu.make_async_copy(moves[n][0], moves[n][1], near_s.at[n])

    for n in range(3):
        local(n).start()

    barrier = pltpu.get_barrier_semaphore()
    group = [peer, to_a, to_b] + x_to[1:] + z_to[1:]
    for device in group:
        pl.semaphore_signal(barrier, inc=1, device_id=device, device_id_type=MESH)
    pl.semaphore_wait(barrier, len(group))

    def rc(src, dst, s, r, to):
        return pltpu.make_async_remote_copy(
            src_ref=src, dst_ref=dst, send_sem=s, recv_sem=r, device_id=to, device_id_type=MESH
        )

    sent = []

    def go(*how):
        copy = rc(*how)
        copy.start()
        sent.append(copy)
        return copy

    mx, mz, ax, az, bz, bx = {}, {}, {}, {}, {}, {}

    def send_az(way, j, h):
        b = at(x + 4 - j, z + (8 - (h - 1) if way == 0 else h - 1))
        az[way, j, h] = go(
            T.at[b] if (j or h > 1) else tok, T.at[b], az_s.at[way, j, h - 1], az_r.at[way, j, h - 1],
            z_to[1] if way == 0 else z_to[7],
        )

    def send_bz(way, h):
        b = at(x, z + (8 - (h - 1) if way == 0 else h - 1))
        bz[way, h] = go(
            C.at[b] if h > 1 else cot, C.at[b], bz_s.at[way, h - 1], bz_r.at[way, h - 1],
            z_to[1] if way == 0 else z_to[7],
        )

    def send_bx(d):
        b = at(x, z + d)
        for n, to in ((0, x_to[1]), (1, x_to[3])):
            bx[n, d] = go(C.at[b] if d else cot, C.at[b], bx_s.at[n, d], bx_r.at[n, d], to)

    def pass_bx(d):
        for n, (off, xx, to) in enumerate(((0, x + 3, x_to[1]), (64, x + 1, x_to[3]))):
            bx[n, d].wait_recv()
            piece = C.at[at(xx, z + d), pl.ds(off, 64)]
            bx[2 + n, d] = go(piece, piece, bx_s.at[2 + n, d], bx_r.at[2 + n, d], to)

    def last(way, j):
        return 4 if (j + way) % 2 == 0 else 3

    M[z, x, 0:8, :] = ids_in[...].astype(F32)
    M[z, x, 8:16, :] = gates_in[...]
    for j in (1, 2, 3):
        mx[j] = go(M.at[z, x], M.at[z, x], mx_s.at[j - 1], mx_r.at[j - 1], x_to[j])
    for j in (1, 2, 3):
        ax[j] = go(tok, T.at[dp], ax_s.at[j - 1], ax_r.at[j - 1], x_to[j])
    send_bz(0, 1)
    send_bz(1, 1)
    send_bx(0)
    for j in (1, 2, 3):
        mx[j].wait_recv()
    for i in range(1, NZ):
        part_m = M.at[z, pl.ds(2 * c, 2)]
        mz[i] = go(part_m, part_m, mz_s.at[i], mz_r.at[i], z_to[i])
    send_az(0, 0, 1)
    send_az(1, 0, 1)
    T[dp] = tok[...]
    C[dp] = cot[...]

    def hop_ax(j):
        ax[j].wait_recv()
        send_az(0, j, 1)
        send_az(1, j, 1)

    def hop_b(h):
        for way in (0, 1):
            if h <= 4 - way:
                bz[way, h].wait_recv()
                if h < 4 - way:
                    send_bz(way, h + 1)
                send_bx(8 - h if way == 0 else h)

    def hop_a(h, *js):
        for j in js:
            for way in (0, 1):
                if h <= last(way, j):
                    az[way, j, h].wait_recv()
                    if h < last(way, j):
                        send_az(way, j, h + 1)

    def places_out():
        for i in range(1, NZ):
            mz[i].wait_recv()
        part_m = M.at[:, pl.ds(2 * c, 2)]
        mz[0] = go(part_m, M2, mz_s.at[0], mz_r.at[0], peer)

    def all_places():
        mz[0].wait_recv()
        MF[:, pl.ds(2 * c, 2)] = M[:, pl.ds(2 * c, 2)]
        MF[:, pl.ds(2 * other, 2)] = M2[...]
        flag = jnp.full((1, 128), plan[dp].astype(F32))
        far = lax.rem(dp + NX * NZ // 2, NX * NZ)
        own_id = (2 * dp + 1).astype(F32)
        star_id = flag * (2 * far + 1).astype(F32) + (1.0 - flag) * own_id
        row_i = lax.broadcasted_iota(jnp.int32, (128, 128), 0)
        col_i = lax.broadcasted_iota(jnp.int32, (128, 128), 1)
        upper = jnp.where(row_i <= col_i, 1.0, 0.0).astype(BF)

        def places(ids, target):
            match = ids == target
            hit = jnp.sum(jnp.where(match, 1.0, 0.0), axis=1)
            return match, jnp.where(hit > 0.0, dot(hit.astype(BF), upper) - 1.0, -1000.0)

        ids = MF[:, :, 0:8, :].reshape(32, 8, 128)
        gates = MF[:, :, 8:16, :].reshape(32, 8, 128)
        for i, target in enumerate(((2 * dp).astype(F32), own_id, star_id[:, None, :])):
            match, rank = places(ids, target)
            RK[i] = rank
            GV[i] = jnp.sum(jnp.where(match, gates, 0.0), axis=1)
        near = MF[:, pl.ds(x, 1), 0:8, :].reshape(8, 8, 128)
        for j in range(4):
            for e in (0, 1):
                _, rank = places(near, (2 * at(x + 4 - j, z) + e).astype(F32))
                RK2[j * 2 + e] = rank

    slot_i = lax.broadcasted_iota(jnp.int32, (48, 256), 0).astype(F32)

    def tiles(body, n=9, width=256):
        def step(i, carry):
            body(pl.ds(pl.multiple_of(i * width, width), width))
            return carry

        lax.fori_loop(0, n, step, 0)

    def pick(ch):
        for d in {(8 - ch) % 8, ch + 1}:
            for n in (2, 3):
                bx[n, d].wait_recv()

        def step(j, carry):
            ba, bb = at(j, z + 8 - ch), at(j, z + 1 + ch)
            ra = lax.rem(z + 8 - ch, NZ) * 4 + j
            rb = lax.rem(z + 1 + ch, NZ) * 4 + j
            ones, scale = [], []
            for i in range(3):
                r0 = RK[i, pl.ds(ra, 1), :]
                r1 = RK[i, pl.ds(rb, 1), :] + 24.0
                eq = slot_i == jnp.concatenate([r0, r1], axis=1)
                g = jnp.concatenate([GV[i, pl.ds(ra, 1), :], GV[i, pl.ds(rb, 1), :]], axis=1)
                ones.append(jnp.where(eq, 1.0, 0.0).astype(BF))
                scale.append(jnp.sum(jnp.where(eq, g, 0.0), axis=1, keepdims=True))
            ones = jnp.concatenate(ones, axis=0)
            scale = jnp.concatenate(scale, axis=0)
            xs = dot(ones, jnp.concatenate([T[ba], T[bb]], axis=0)).astype(BF)
            gs = (dot(ones, jnp.concatenate([C[ba], C[bb]], axis=0)) * scale).astype(BF)
            rows = pl.ds(pl.multiple_of(48 * j, 16), 48)
            for i in range(3):
                X[i, ch, rows, :] = xs[48 * i : 48 * i + 48]
                G[i, ch, rows, :] = gs[48 * i : 48 * i + 48]
            return carry

        lax.fori_loop(0, 4, step, 0)

    cs, sy = {}, {}

    def project(ch):
        for own in (False, True):
            e = c if own else other
            for kind, w in enumerate((wg, wu, wd)):
                for n in range(0, FF, 256):
                    if kind < 2:
                        res = dot(X[e, ch], w[e, :, n : n + 256])
                    else:
                        res = dot_nt(G[e, ch], w[e, n : n + 256, :])
                    col = slice(kind * FF + n, kind * FF + n + 256)
                    if own:
                        H[ch % 2, :, col] = res
                    else:
                        CS[ch, :, col] = res.astype(BF)
            if not own:
                cs[ch] = go(CS.at[ch], CR.at[ch], cs_s.at[ch], cs_r.at[ch], peer)

    def part(ch, yy, col):
        rows = pl.ds(pl.multiple_of(yy * 48, 16), 48)
        return H[ch % 2, rows, col] + CR[ch, rows, col].astype(F32)

    def message(ch, m, yy, to, plus=None):
        def body(col):
            v = part(ch, yy, col)
            if plus is not None:
                v = v + RY[ch, plus, :, col].astype(F32)
            SY[ch, m, :, col] = v.astype(BF)

        tiles(body)
        sy[ch, m] = go(SY.at[ch, m], RY.at[ch, m], sy_s.at[ch, m], sy_r.at[ch, m], to)

    def ring_one(ch):
        cs[ch].wait_recv()
        message(ch, 0, y_opp, to_a)
        message(ch, 1, y_b, to_b)

    def ring_two(ch):
        sy[ch, 0].wait_recv()
        message(ch, 2, y_a, to_a, plus=0)

    swaps = lambda ch: rc(PS.at[ch], PR.at[ch], ps_s.at[ch], ps_r.at[ch], x_to[2])

    def activate(ch):
        sy[ch, 1].wait_recv()
        sy[ch, 2].wait_recv()

        def body(i, carry):
            cols = [pl.ds(pl.multiple_of(k * FF + i * 128, 128), 128) for k in range(3)]

            def total(col):
                v = part(ch, y, col)
                return v + RY[ch, 1, :, col].astype(F32) + RY[ch, 2, :, col].astype(F32)

            gate, up, back = [total(col) for col in cols]
            sig = jax.nn.sigmoid(gate)
            silu = gate * sig
            PS[ch, :, cols[0]] = (silu * up).astype(BF)
            PS[ch, :, cols[1]] = (back * up * sig * (1.0 + gate * (1.0 - sig))).astype(BF)
            PS[ch, :, cols[2]] = (back * silu).astype(BF)
            return carry

        lax.fori_loop(0, 6, body, 0)

        @pl.when(c == 1)
        def _():
            swaps(ch).start()
            AH[ch, y] = PS[ch, :, FF:]
            for n, to in ((0, to_a), (1, to_b), (2, peer)):
                ah(ch, n, y, to).start()

        @pl.when(c == 0)
        def _():
            AB[0, ch, y] = PS[ch]
            for n, to in ((0, to_a), (1, to_b), (2, peer)):
                ag(ch, n, y, to).start()

    def ag(ch, n, yy, to):
        block = AB.at[c, ch, yy]
        return rc(block, block, ag_s.at[ch, n], ag_r.at[ch, n], to)

    def ah(ch, n, yy, to):
        block = AH.at[ch, yy]
        return rc(block, block, ah_s.at[ch, n], ah_r.at[ch, n], to)

    def choose(ch):
        @pl.when(c == 1)
        def _():
            swaps(ch).wait_recv()

            def body(col):
                keep = jnp.full((48, 256), plan[dp].astype(F32)) > 0.5
                v = jnp.where(keep, PR[ch, :, col].astype(F32), PS[ch, :, col].astype(F32))
                AB[1, ch, y, :, col] = v.astype(BF)

            tiles(body)
            for n, to in ((0, to_a), (1, to_b), (2, peer)):
                ag(ch, n, y, to).start()

    def pass_on(block, ch):
        block(ch, 0, y_b, to_a).wait_recv()
        block(ch, 3, y_b, to_a).start()
        block(ch, 4, y_b, peer).start()
        block(ch, 1, y_a, to_b).wait_recv()
        block(ch, 5, y_a, peer).start()

    def pass_end(block, ch):
        block(ch, 3, y_opp, to_a).wait_recv()
        block(ch, 6, y_opp, peer).start()

    def on_cores(zero, one):
        if zero is not None:
            pl.when(c == 0)(zero)
        pl.when(c == 1)(one)

    def tok_pass(ch):
        on_cores(lambda: pass_on(ag, ch), lambda: pass_on(ah, ch))

    def tok_end(ch):
        on_cores(lambda: pass_end(ag, ch), lambda: pass_end(ah, ch))

    def peer_in(block, ch):
        for n in (2, 4, 5, 6):
            block(ch, n, y, peer).wait_recv()

    def tok_done(ch):
        on_cores(lambda: peer_in(ah, ch), lambda: peer_in(ag, ch))

    def star_pass(ch):
        on_cores(None, lambda: pass_on(ag, ch))

    def star_end(ch):
        on_cores(None, lambda: pass_end(ag, ch))

    def star_done(ch):
        pl.when(c == 0)(lambda: peer_in(ag, ch))

    rx = {}

    def back_rows(ch):
        for e in (0, 1):
            gd = (AB[0, ch, :, :, FF : 2 * FF] if e == 0 else AH[ch, :, :, :FF]).reshape(192, FF)
            ud = (AB[0, ch, :, :, 2 * FF :] if e == 0 else AH[ch, :, :, FF:]).reshape(192, FF)
            for n in (0, 256):
                res = dot_nt(gd, wg[e, n : n + 256, :]) + dot_nt(ud, wu[e, n : n + 256, :])
                R[ch, e, :, :, n : n + 256] = res.astype(BF).reshape(4, 48, 256)
        for j in (1, 2, 3):
            rx[ch, j] = go(R.at[ch, :, lax.rem(x + j, NX)], RB.at[ch, j], rx_s.at[ch, j - 1], rx_r.at[ch, j - 1], x_to[j])

    rz = {}

    def spread(ch):
        for j in (1, 2, 3):
            rx[ch, j].wait_recv()
        za, zb = lax.rem(z + 8 - ch, NZ), lax.rem(z + 1 + ch, NZ)
        pieces = []
        for s in range(8):
            r0 = RK2[s, pl.ds(za, 1), :]
            r1 = RK2[s, pl.ds(zb, 1), :] + 24.0
            pieces.append(jnp.where(slot_i == jnp.concatenate([r0, r1], axis=1), 1.0, 0.0).astype(BF))
        own = dot_tn(jnp.concatenate(pieces[:2], axis=0), R[ch, :, pl.ds(x, 1)].reshape(96, 512))
        rest = dot_tn(jnp.concatenate(pieces[2:], axis=0), RB[ch, 1:].reshape(288, 512))
        v = own + rest
        for i, d in ((0, (8 - ch) % 8), (1, ch + 1)):
            block = v[128 * i : 128 * i + 128]
            if d == 0:
                OWN[...] = block
            else:
                DS[d] = block.astype(BF)
                rz[d] = go(DS.at[d], ZR.at[d], rz_s.at[d], rz_r.at[d], z_to[d])

    def input_grads(slot, i):
        def inputs(n, carry):
            d = pl.ds(pl.multiple_of(n * 256, 256), 256)
            xs = X[i, :, :, d].reshape(FF, 256)
            for k, out in ((1, gg_o), (2, ug_o)):
                act = AB[slot, :, :, :, k * FF : (k + 1) * FF].reshape(FF, FF)
                out[slot, d, :] = dot_tn(xs, act).astype(BF)
            return carry

        lax.fori_loop(0, 2, inputs, 0)

    def hidden_grads(slot, i):
        def hidden(n, carry):
            f = pl.ds(pl.multiple_of(n * 256, 256), 256)
            hid = AB[slot, :, :, :, f].reshape(FF, 256)
            dg_o[slot, f, :] = dot_tn(hid, G[i].reshape(FF, 512)).astype(BF)
            return carry

        lax.fori_loop(0, 3, hidden, 0)

    def forward(ch):
        pick(ch)
        project(ch)

    hop_ax(1)
    hop_ax(3)
    hop_b(1)
    hop_ax(2)
    pass_bx(0)
    hop_a(1, 0)
    hop_b(2)
    hop_a(1, 1)
    places_out()
    pass_bx(7)
    pass_bx(1)
    hop_a(1, 3)
    hop_b(3)
    for n in range(3):
        local(n).wait()
    all_places()
    hop_a(1, 2)
    forward(0)
    pass_bx(6)
    pass_bx(2)
    hop_a(2, 0, 1)
    hop_b(4)
    ring_one(0)
    hop_a(2, 3, 2)
    pass_bx(5)
    pass_bx(3)
    ring_two(0)
    forward(1)
    pass_bx(4)
    activate(0)
    ring_one(1)
    tok_pass(0)
    ring_two(1)
    hop_a(3, 0, 1, 3, 2)
    forward(2)
    tok_end(0)
    activate(1)
    ring_one(2)
    choose(0)
    tok_done(0)
    back_rows(0)
    tok_pass(1)
    ring_two(2)
    hop_a(4, 0, 1, 3, 2)
    forward(3)
    tok_end(1)
    activate(2)
    ring_one(3)
    star_pass(0)
    choose(1)
    tok_done(1)
    back_rows(1)
    spread(0)
    tok_pass(2)
    ring_two(3)
    star_end(0)
    star_pass(1)
    choose(2)
    tok_end(2)
    activate(3)
    tok_done(2)
    back_rows(2)
    spread(1)
    tok_pass(3)
    star_end(1)
    star_pass(2)
    choose(3)
    spread(2)
    tok_end(3)
    star_end(2)
    tok_done(3)
    back_rows(3)
    star_pass(3)
    hidden_grads(0, 0)
    local(8).start()
    spread(3)
    star_end(3)
    input_grads(0, 0)
    local(3).start()
    local(4).start()
    for ch in range(4):
        star_done(ch)
    hidden_grads(1, 2)
    local(5).start()
    input_grads(1, 2)
    local(6).start()
    local(7).start()

    total = OWN[...]
    for d in (1, 7, 2, 6, 3, 5, 4):
        rz[d].wait_recv()
        total = total + ZR[d].astype(F32)
    tg_o[...] = total.astype(BF)
    local(9).start()
    for n in range(3, 10):
        local(n).wait()
    for copy in sent:
        copy.wait_send()
    for ch in range(4):
        for n in range(7):
            ag(ch, n, y, peer).wait_send()

        @pl.when(c == 1)
        def _():
            swaps(ch).wait_send()
            for n in range(7):
                ah(ch, n, y, peer).wait_send()


def hand_out(tg, gg, ug, dg, tg_o, gg_o, ug_o, dg_o, tg_v, gg_v, ug_v, dg_v, sem):
    steps = [(tg, tg_v, tg_o)]
    for src, mid, dst in ((gg, gg_v, gg_o), (ug, ug_v, ug_o), (dg, dg_v, dg_o)):
        steps += [(src.at[e], mid.at[e], dst.at[e]) for e in (0, 1)]
    first = [pltpu.make_async_copy(a, b, sem.at[0, n]) for n, (a, b, _) in enumerate(steps)]
    then = [pltpu.make_async_copy(b, d, sem.at[1, n]) for n, (_, b, d) in enumerate(steps)]
    for copy in first:
        copy.start()
    for one, two in zip(first, then):
        one.wait()
        two.start()
    for copy in then:
        copy.wait()


def shards(tokens, cotangent, expert_ids, gate_values, swap_plan, gate_weight, up_weight, down_weight):
    vmem = pl.BlockSpec(memory_space=pltpu.VMEM)
    hbm = pl.BlockSpec(memory_space=pl.ANY)
    dma = lambda *shape: [pltpu.SemaphoreType.DMA(shape), pltpu.SemaphoreType.DMA(shape)]
    w = 3 * FF
    outs = pl.pallas_call(
        kernel,
        out_shape=(
            jax.ShapeDtypeStruct(tokens.shape, BF),
            jax.ShapeDtypeStruct(gate_weight.shape, BF),
            jax.ShapeDtypeStruct(up_weight.shape, BF),
            jax.ShapeDtypeStruct(down_weight.shape, BF),
        ),
        in_specs=[pl.BlockSpec(memory_space=pltpu.SMEM)] + [vmem] * 4 + [hbm] * 3,
        out_specs=(hbm,) * 4,
        scratch_shapes=[
            pltpu.VMEM(gate_weight.shape, BF),
            pltpu.VMEM(up_weight.shape, BF),
            pltpu.VMEM(down_weight.shape, BF),
            pltpu.VMEM(tokens.shape, BF),
            pltpu.VMEM(gate_weight.shape, BF),
            pltpu.VMEM(up_weight.shape, BF),
            pltpu.VMEM(down_weight.shape, BF),
            pltpu.SemaphoreType.DMA((10,)),
            pltpu.VMEM((32, 128, 512), BF),
            pltpu.VMEM((32, 128, 512), BF),
            pltpu.VMEM((8, 4, 16, 128), F32),
            pltpu.VMEM((8, 2, 16, 128), F32),
            pltpu.VMEM((8, 4, 16, 128), F32),
            pltpu.VMEM((3, 4, 192, 512), BF),
            pltpu.VMEM((3, 4, 192, 512), BF),
            pltpu.VMEM((3, 32, 128), F32),
            pltpu.VMEM((3, 32, 128), F32),
            pltpu.VMEM((8, 8, 128), F32),
            pltpu.VMEM((4, 192, w), BF),
            pltpu.VMEM((4, 192, w), BF),
            pltpu.VMEM((2, 192, w), F32),
            pltpu.VMEM((4, 3, 48, w), BF),
            pltpu.VMEM((4, 3, 48, w), BF),
            pltpu.VMEM((4, 48, w), BF),
            pltpu.VMEM((4, 48, w), BF),
            pltpu.VMEM((2, 4, 4, 48, w), BF),
            pltpu.VMEM((4, 4, 48, 2 * FF), BF),
            pltpu.VMEM((4, 2, 4, 48, 512), BF),
            pltpu.VMEM((4, 4, 2, 48, 512), BF),
            pltpu.VMEM((8, 128, 512), BF),
            pltpu.VMEM((8, 128, 512), BF),
            pltpu.VMEM((128, 512), F32),
        ]
        + dma(3)
        + dma(8)
        + dma(3)
        + dma(2, 4, 4)
        + dma(2, 4)
        + dma(4, 8)
        + dma(4)
        + dma(4, 3)
        + dma(4)
        + dma(4, 7)
        + dma(4, 7)
        + dma(4, 3)
        + dma(8),
        compiler_params=pltpu.CompilerParams(
            collective_id=0, has_side_effects=True, vmem_limit_bytes=62 << 20
        ),
        cost_estimate=pl.CostEstimate(flops=10_000_000_000, bytes_accessed=10_000_000, transcendentals=0),
        name="expert_layer",
    )(
        swap_plan, tokens, cotangent, expert_ids.T, gate_values.T, gate_weight, up_weight, down_weight
    )
    return pl.pallas_call(
        hand_out,
        out_shape=tuple(jax.ShapeDtypeStruct(o.shape, o.dtype) for o in outs),
        in_specs=[hbm] * 4,
        out_specs=(hbm,) * 4,
        scratch_shapes=[pltpu.VMEM(o.shape, o.dtype) for o in outs] + [pltpu.SemaphoreType.DMA((2, 7))],
        name="hand_out",
    )(*outs)


def solution(mesh):
    return jax.shard_map(
        shards,
        mesh=mesh,
        in_specs=(
            P("dp", "expert"),
            P("dp", "expert"),
            P("dp", None),
            P("dp", None),
            P(),
            P("dp", "expert", None),
            P("dp", "expert", None),
            P("dp", None, "expert"),
        ),
        out_specs=(
            P("dp", "expert"),
            P("dp", "expert", None),
            P("dp", "expert", None),
            P("dp", None, "expert"),
        ),
        check_vma=False,
    )
```

```python
import functools

import jax
import jax.numpy as jnp
from jax import lax
from jax.experimental import pallas as pl
from jax.experimental.pallas import tpu as pltpu
from jax.sharding import PartitionSpec as P

BF = jnp.bfloat16
F32 = jnp.float32
MESH = pl.DeviceIdType.MESH
NX, NZ, NY = 4, 8, 4
FF = 768
PAIRS = ((7, 1), (6, 2), (5, 3), (0, 4))


def dot(a, b):
    return lax.dot_general(a, b, (((1,), (0,)), ((), ())), preferred_element_type=F32)


def dot_nt(a, b):
    return lax.dot_general(a, b, (((1,), (1,)), ((), ())), preferred_element_type=F32)


def dot_tn(a, b):
    return lax.dot_general(a, b, (((0,), (0,)), ((), ())), preferred_element_type=F32)


def kernel(
    plan, tok, cot, ids_in, gates_in, wg_in, wu_in, wd_in,
    tg_out, gg_out, ug_out, dg_out,
    wg, wu, wd, tg_o, gg_o, ug_o, dg_o, near_s,
    T, C, M, M2, MF, X, G, RK, GV, RK2, CS, CR, H, SY, RY, PS, PR, AB, AH, R, RB, DS, ZR, OWN,
    mx_s, mx_r, mz_s, mz_r, ax_s, ax_r, az_s, az_r, bz_s, bz_r, bx_s, bx_r, cs_s, cs_r,
    sy_s, sy_r, ps_s, ps_r, ag_s, ag_r, ah_s, ah_r, rx_s, rx_r, rz_s, rz_r,
):
    dp = lax.axis_index("dp")
    ex = lax.axis_index("expert")
    x, z = lax.div(dp, NZ), lax.rem(dp, NZ)
    y, c = lax.div(ex, 2), lax.rem(ex, 2)
    other = 1 - c

    def at(xx, zz):
        return lax.rem(xx, NX) * NZ + lax.rem(zz, NZ)

    turn = 1 + 2 * c
    y_a, y_b, y_opp = lax.rem(y + turn, NY), lax.rem(y + NY - turn, NY), lax.rem(y + 2, NY)
    peer = (dp, y * 2 + other)
    to_a, to_b = (dp, y_a * 2 + c), (dp, y_b * 2 + c)
    x_to = [None] + [(at(x + j, z), ex) for j in (1, 2, 3)]
    z_to = [None] + [(at(x, z + i), ex) for i in range(1, NZ)]

    moves = [(wg_in, wg), (wu_in, wu), (wd_in, wd)]
    moves += [(gg_o.at[0], gg_out.at[0]), (ug_o.at[0], ug_out.at[0]), (dg_o.at[1], dg_out.at[1])]
    moves += [(gg_o.at[1], gg_out.at[1]), (ug_o.at[1], ug_out.at[1]), (dg_o.at[0], dg_out.at[0])]
    moves += [(tg_o, tg_out)]

    def local(n):
        return pltpu.make_async_copy(moves[n][0], moves[n][1], near_s.at[n])

    for n in range(3):
        local(n).start()

    barrier = pltpu.get_barrier_semaphore()
    group = [peer, to_a, to_b] + x_to[1:] + z_to[1:]
    for device in group:
        pl.semaphore_signal(barrier, inc=1, device_id=device, device_id_type=MESH)
    pl.semaphore_wait(barrier, len(group))

    def rc(src, dst, s, r, to):
        return pltpu.make_async_remote_copy(
            src_ref=src, dst_ref=dst, send_sem=s, recv_sem=r, device_id=to, device_id_type=MESH
        )

    sent = []

    def go(*how):
        copy = rc(*how)
        copy.start()
        sent.append(copy)
        return copy

    mx, mz, ax, az, bz, bx = {}, {}, {}, {}, {}, {}

    def send_az(way, j, h):
        b = at(x + 4 - j, z + (8 - (h - 1) if way == 0 else h - 1))
        az[way, j, h] = go(
            T.at[b] if (j or h > 1) else tok, T.at[b], az_s.at[way, j, h - 1], az_r.at[way, j, h - 1],
            z_to[1] if way == 0 else z_to[7],
        )

    def send_bz(way, h):
        b = at(x, z + (8 - (h - 1) if way == 0 else h - 1))
        bz[way, h] = go(
            C.at[b] if h > 1 else cot, C.at[b], bz_s.at[way, h - 1], bz_r.at[way, h - 1],
            z_to[1] if way == 0 else z_to[7],
        )

    def send_bx(d):
        b = at(x, z + d)
        for n, to in ((0, x_to[1]), (1, x_to[3])):
            bx[n, d] = go(C.at[b] if d else cot, C.at[b], bx_s.at[n, d], bx_r.at[n, d], to)

    def pass_bx(d):
        for n, (off, xx, to) in enumerate(((0, x + 3, x_to[1]), (64, x + 1, x_to[3]))):
            bx[n, d].wait_recv()
            piece = C.at[at(xx, z + d), pl.ds(off, 64)]
            bx[2 + n, d] = go(piece, piece, bx_s.at[2 + n, d], bx_r.at[2 + n, d], to)

    def last(way, j):
        return 4 if (j + way) % 2 == 0 else 3

    M[z, x, 0:8, :] = ids_in[...].astype(F32)
    M[z, x, 8:16, :] = gates_in[...]
    for j in (1, 2, 3):
        mx[j] = go(M.at[z, x], M.at[z, x], mx_s.at[j - 1], mx_r.at[j - 1], x_to[j])
    for j in (1, 2, 3):
        ax[j] = go(tok, T.at[dp], ax_s.at[j - 1], ax_r.at[j - 1], x_to[j])
    send_bz(0, 1)
    send_bz(1, 1)
    send_bx(0)
    for j in (1, 2, 3):
        mx[j].wait_recv()
    for i in range(1, NZ):
        part_m = M.at[z, pl.ds(2 * c, 2)]
        mz[i] = go(part_m, part_m, mz_s.at[i], mz_r.at[i], z_to[i])
    send_az(0, 0, 1)
    send_az(1, 0, 1)
    T[dp] = tok[...]
    C[dp] = cot[...]

    def hop_ax(j):
        ax[j].wait_recv()
        send_az(0, j, 1)
        send_az(1, j, 1)

    def hop_b(h):
        for way in (0, 1):
            if h <= 4 - way:
                bz[way, h].wait_recv()
                if h < 4 - way:
                    send_bz(way, h + 1)
                send_bx(8 - h if way == 0 else h)

    def hop_a(h, *js):
        for j in js:
            for way in (0, 1):
                if h <= last(way, j):
                    az[way, j, h].wait_recv()
                    if h < last(way, j):
                        send_az(way, j, h + 1)

    def places_out():
        for i in range(1, NZ):
            mz[i].wait_recv()
        part_m = M.at[:, pl.ds(2 * c, 2)]
        mz[0] = go(part_m, M2, mz_s.at[0], mz_r.at[0], peer)

    def all_places():
        mz[0].wait_recv()
        MF[:, pl.ds(2 * c, 2)] = M[:, pl.ds(2 * c, 2)]
        MF[:, pl.ds(2 * other, 2)] = M2[...]
        flag = jnp.full((1, 128), plan[dp].astype(F32))
        far = lax.rem(dp + NX * NZ // 2, NX * NZ)
        own_id = (2 * dp + 1).astype(F32)
        star_id = flag * (2 * far + 1).astype(F32) + (1.0 - flag) * own_id
        row_i = lax.broadcasted_iota(jnp.int32, (128, 128), 0)
        col_i = lax.broadcasted_iota(jnp.int32, (128, 128), 1)
        upper = jnp.where(row_i <= col_i, 1.0, 0.0).astype(BF)

        def places(ids, target):
            match = ids == target
            hit = jnp.sum(jnp.where(match, 1.0, 0.0), axis=1)
            return match, jnp.where(hit > 0.0, dot(hit.astype(BF), upper) - 1.0, -1000.0)

        ids = MF[:, :, 0:8, :].reshape(32, 8, 128)
        gates = MF[:, :, 8:16, :].reshape(32, 8, 128)
        for i, target in enumerate(((2 * dp).astype(F32), own_id, star_id[:, None, :])):
            match, rank = places(ids, target)
            RK[i] = rank
            GV[i] = jnp.sum(jnp.where(match, gates, 0.0), axis=1)
        near = MF[:, pl.ds(x, 1), 0:8, :].reshape(8, 8, 128)
        for j in range(4):
            for e in (0, 1):
                _, rank = places(near, (2 * at(x + 4 - j, z) + e).astype(F32))
                RK2[j * 2 + e] = rank

    slot_i = lax.broadcasted_iota(jnp.int32, (48, 256), 0).astype(F32)

    def tiles(body, n=9, width=256):
        def step(i, carry):
            body(pl.ds(pl.multiple_of(i * width, width), width))
            return carry

        lax.fori_loop(0, n, step, 0)

    def pick(ch):
        da, db = PAIRS[ch]
        for d in (da, db):
            for n in (2, 3):
                bx[n, d].wait_recv()

        def step(j, carry):
            ba, bb = at(j, z + da), at(j, z + db)
            ra = lax.rem(z + da, NZ) * 4 + j
            rb = lax.rem(z + db, NZ) * 4 + j
            ones, scale = [], []
            for i in range(3):
                r0 = RK[i, pl.ds(ra, 1), :]
                r1 = RK[i, pl.ds(rb, 1), :] + 24.0
                eq = slot_i == jnp.concatenate([r0, r1], axis=1)
                g = jnp.concatenate([GV[i, pl.ds(ra, 1), :], GV[i, pl.ds(rb, 1), :]], axis=1)
                ones.append(jnp.where(eq, 1.0, 0.0).astype(BF))
                scale.append(jnp.sum(jnp.where(eq, g, 0.0), axis=1, keepdims=True))
            ones = jnp.concatenate(ones, axis=0)
            scale = jnp.concatenate(scale, axis=0)
            xs = dot(ones, jnp.concatenate([T[ba], T[bb]], axis=0)).astype(BF)
            gs = (dot(ones, jnp.concatenate([C[ba], C[bb]], axis=0)) * scale).astype(BF)
            rows = pl.ds(pl.multiple_of(48 * j, 16), 48)
            for i in range(3):
                X[i, ch, rows, :] = xs[48 * i : 48 * i + 48]
                G[i, ch, rows, :] = gs[48 * i : 48 * i + 48]
            return carry

        lax.fori_loop(0, 4, step, 0)

    cs, sy = {}, {}

    def project(ch):
        for own in (False, True):
            e = c if own else other
            for kind, w in enumerate((wg, wu, wd)):
                for n in range(0, FF, 256):
                    if kind < 2:
                        res = dot(X[e, ch], w[e, :, n : n + 256])
                    else:
                        res = dot_nt(G[e, ch], w[e, n : n + 256, :])
                    col = slice(kind * FF + n, kind * FF + n + 256)
                    if own:
                        H[ch % 2, :, col] = res
                    else:
                        CS[ch, :, col] = res.astype(BF)
            if not own:
                cs[ch] = go(CS.at[ch], CR.at[ch], cs_s.at[ch], cs_r.at[ch], peer)

    def part(ch, yy, col):
        rows = pl.ds(pl.multiple_of(yy * 48, 16), 48)
        return H[ch % 2, rows, col] + CR[ch, rows, col].astype(F32)

    def message(ch, m, yy, to, plus=None):
        def body(col):
            v = part(ch, yy, col)
            if plus is not None:
                v = v + RY[ch, plus, :, col].astype(F32)
            SY[ch, m, :, col] = v.astype(BF)

        tiles(body)
        sy[ch, m] = go(SY.at[ch, m], RY.at[ch, m], sy_s.at[ch, m], sy_r.at[ch, m], to)

    def ring_one(ch):
        cs[ch].wait_recv()
        message(ch, 0, y_opp, to_a)
        message(ch, 1, y_b, to_b)

    def ring_two(ch):
        sy[ch, 0].wait_recv()
        message(ch, 2, y_a, to_a, plus=0)

    swaps = lambda ch: rc(PS.at[ch], PR.at[ch], ps_s.at[ch], ps_r.at[ch], x_to[2])

    def activate(ch):
        sy[ch, 1].wait_recv()
        sy[ch, 2].wait_recv()

        def body(i, carry):
            cols = [pl.ds(pl.multiple_of(k * FF + i * 128, 128), 128) for k in range(3)]

            def total(col):
                v = part(ch, y, col)
                return v + RY[ch, 1, :, col].astype(F32) + RY[ch, 2, :, col].astype(F32)

            gate, up, back = [total(col) for col in cols]
            sig = jax.nn.sigmoid(gate)
            silu = gate * sig
            PS[ch, :, cols[0]] = (silu * up).astype(BF)
            PS[ch, :, cols[1]] = (back * up * sig * (1.0 + gate * (1.0 - sig))).astype(BF)
            PS[ch, :, cols[2]] = (back * silu).astype(BF)
            return carry

        lax.fori_loop(0, 6, body, 0)

        @pl.when(c == 1)
        def _():
            swaps(ch).start()
            AH[ch, y] = PS[ch, :, FF:]
            for n, to in ((0, to_a), (1, to_b), (2, peer)):
                ah(ch, n, y, to).start()

        @pl.when(c == 0)
        def _():
            AB[0, ch, y] = PS[ch]
            for n, to in ((0, to_a), (1, to_b), (2, peer)):
                ag(ch, n, y, to).start()

    def ag(ch, n, yy, to):
        block = AB.at[c, ch, yy]
        return rc(block, block, ag_s.at[ch, n], ag_r.at[ch, n], to)

    def ah(ch, n, yy, to):
        block = AH.at[ch, yy]
        return rc(block, block, ah_s.at[ch, n], ah_r.at[ch, n], to)

    def choose(ch):
        @pl.when(c == 1)
        def _():
            swaps(ch).wait_recv()

            def body(col):
                keep = jnp.full((48, 256), plan[dp].astype(F32)) > 0.5
                v = jnp.where(keep, PR[ch, :, col].astype(F32), PS[ch, :, col].astype(F32))
                AB[1, ch, y, :, col] = v.astype(BF)

            tiles(body)
            for n, to in ((0, to_a), (1, to_b), (2, peer)):
                ag(ch, n, y, to).start()

    def pass_on(block, ch):
        block(ch, 0, y_b, to_a).wait_recv()
        block(ch, 3, y_b, to_a).start()
        block(ch, 4, y_b, peer).start()
        block(ch, 1, y_a, to_b).wait_recv()
        block(ch, 5, y_a, peer).start()

    def pass_end(block, ch):
        block(ch, 3, y_opp, to_a).wait_recv()
        block(ch, 6, y_opp, peer).start()

    def on_cores(zero, one):
        if zero is not None:
            pl.when(c == 0)(zero)
        pl.when(c == 1)(one)

    def tok_pass(ch):
        on_cores(lambda: pass_on(ag, ch), lambda: pass_on(ah, ch))

    def tok_end(ch):
        on_cores(lambda: pass_end(ag, ch), lambda: pass_end(ah, ch))

    def peer_in(block, ch):
        for n in (2, 4, 5, 6):
            block(ch, n, y, peer).wait_recv()

    def tok_done(ch):
        on_cores(lambda: peer_in(ah, ch), lambda: peer_in(ag, ch))

    def star_pass(ch):
        on_cores(None, lambda: pass_on(ag, ch))

    def star_end(ch):
        on_cores(None, lambda: pass_end(ag, ch))

    def star_done(ch):
        pl.when(c == 0)(lambda: peer_in(ag, ch))

    rx = {}

    def back_rows(ch):
        for e in (0, 1):
            gd = (AB[0, ch, :, :, FF : 2 * FF] if e == 0 else AH[ch, :, :, :FF]).reshape(192, FF)
            ud = (AB[0, ch, :, :, 2 * FF :] if e == 0 else AH[ch, :, :, FF:]).reshape(192, FF)
            for n in (0, 256):
                res = dot_nt(gd, wg[e, n : n + 256, :]) + dot_nt(ud, wu[e, n : n + 256, :])
                R[ch, e, :, :, n : n + 256] = res.astype(BF).reshape(4, 48, 256)
        for j in (1, 2, 3):
            rx[ch, j] = go(R.at[ch, :, lax.rem(x + j, NX)], RB.at[ch, j], rx_s.at[ch, j - 1], rx_r.at[ch, j - 1], x_to[j])

    rz = {}

    def spread(ch):
        for j in (1, 2, 3):
            rx[ch, j].wait_recv()
        da, db = PAIRS[ch]
        za, zb = lax.rem(z + da, NZ), lax.rem(z + db, NZ)
        pieces = []
        for s in range(8):
            r0 = RK2[s, pl.ds(za, 1), :]
            r1 = RK2[s, pl.ds(zb, 1), :] + 24.0
            pieces.append(jnp.where(slot_i == jnp.concatenate([r0, r1], axis=1), 1.0, 0.0).astype(BF))
        own = dot_tn(jnp.concatenate(pieces[:2], axis=0), R[ch, :, pl.ds(x, 1)].reshape(96, 512))
        rest = dot_tn(jnp.concatenate(pieces[2:], axis=0), RB[ch, 1:].reshape(288, 512))
        v = own + rest
        for i, d in ((1, db), (0, da)):
            block = v[128 * i : 128 * i + 128]
            if d == 0:
                OWN[...] = block
            else:
                DS[d] = block.astype(BF)
                rz[d] = go(DS.at[d], ZR.at[d], rz_s.at[d], rz_r.at[d], z_to[d])

    def input_grads(slot, i):
        def inputs(n, carry):
            d = pl.ds(pl.multiple_of(n * 256, 256), 256)
            xs = X[i, :, :, d].reshape(FF, 256)
            for k, out in ((1, gg_o), (2, ug_o)):
                act = AB[slot, :, :, :, k * FF : (k + 1) * FF].reshape(FF, FF)
                out[slot, d, :] = dot_tn(xs, act).astype(BF)
            return carry

        lax.fori_loop(0, 2, inputs, 0)

    def hidden_grads(slot, i):
        def hidden(n, carry):
            f = pl.ds(pl.multiple_of(n * 256, 256), 256)
            hid = AB[slot, :, :, :, f].reshape(FF, 256)
            dg_o[slot, f, :] = dot_tn(hid, G[i].reshape(FF, 512)).astype(BF)
            return carry

        lax.fori_loop(0, 3, hidden, 0)

    def forward(ch):
        pick(ch)
        project(ch)

    hop_ax(1)
    hop_ax(3)
    hop_b(1)
    hop_ax(2)
    pass_bx(0)
    hop_a(1, 0)
    hop_b(2)
    hop_a(1, 1)
    places_out()
    pass_bx(7)
    pass_bx(1)
    hop_a(1, 3)
    hop_b(3)
    for n in range(3):
        local(n).wait()
    all_places()
    hop_a(1, 2)
    forward(0)
    pass_bx(6)
    pass_bx(2)
    hop_a(2, 0, 1)
    hop_b(4)
    ring_one(0)
    hop_a(2, 3, 2)
    pass_bx(5)
    pass_bx(3)
    ring_two(0)
    forward(1)
    pass_bx(4)
    activate(0)
    ring_one(1)
    tok_pass(0)
    ring_two(1)
    hop_a(3, 0, 1, 3, 2)
    forward(2)
    tok_end(0)
    activate(1)
    ring_one(2)
    choose(0)
    tok_done(0)
    back_rows(0)
    tok_pass(1)
    ring_two(2)
    hop_a(4, 0, 1, 3, 2)
    forward(3)
    tok_end(1)
    activate(2)
    ring_one(3)
    star_pass(0)
    choose(1)
    tok_done(1)
    back_rows(1)
    spread(0)
    tok_pass(2)
    ring_two(3)
    tok_end(2)
    star_end(0)
    activate(3)
    star_pass(1)
    choose(2)
    tok_done(2)
    back_rows(2)
    spread(1)
    tok_pass(3)
    star_end(1)
    choose(3)
    tok_end(3)
    star_pass(2)
    spread(2)
    tok_done(3)
    back_rows(3)
    star_end(2)
    star_pass(3)
    hidden_grads(0, 0)
    local(8).start()
    spread(3)
    star_end(3)
    input_grads(0, 0)
    local(3).start()
    local(4).start()
    for ch in range(4):
        star_done(ch)
    hidden_grads(1, 2)
    local(5).start()
    input_grads(1, 2)
    local(6).start()
    local(7).start()

    total = OWN[...]
    for d in (1, 7, 2, 6, 3, 5, 4):
        rz[d].wait_recv()
        total = total + ZR[d].astype(F32)
    tg_o[...] = total.astype(BF)
    local(9).start()
    for n in range(3, 10):
        local(n).wait()
    for copy in sent:
        copy.wait_send()
    for ch in range(4):
        for n in range(7):
            ag(ch, n, y, peer).wait_send()

        @pl.when(c == 1)
        def _():
            swaps(ch).wait_send()
            for n in range(7):
                ah(ch, n, y, peer).wait_send()


def hand_out(tg, gg, ug, dg, tg_o, gg_o, ug_o, dg_o, tg_v, gg_v, ug_v, dg_v, sem):
    steps = [(tg, tg_v, tg_o)]
    for src, mid, dst in ((gg, gg_v, gg_o), (ug, ug_v, ug_o), (dg, dg_v, dg_o)):
        steps += [(src.at[e], mid.at[e], dst.at[e]) for e in (0, 1)]
    first = [pltpu.make_async_copy(a, b, sem.at[0, n]) for n, (a, b, _) in enumerate(steps)]
    then = [pltpu.make_async_copy(b, d, sem.at[1, n]) for n, (_, b, d) in enumerate(steps)]
    for copy in first:
        copy.start()
    for one, two in zip(first, then):
        one.wait()
        two.start()
    for copy in then:
        copy.wait()


def shards(tokens, cotangent, expert_ids, gate_values, swap_plan, gate_weight, up_weight, down_weight):
    vmem = pl.BlockSpec(memory_space=pltpu.VMEM)
    hbm = pl.BlockSpec(memory_space=pl.ANY)
    dma = lambda *shape: [pltpu.SemaphoreType.DMA(shape), pltpu.SemaphoreType.DMA(shape)]
    w = 3 * FF
    outs = pl.pallas_call(
        kernel,
        out_shape=(
            jax.ShapeDtypeStruct(tokens.shape, BF),
            jax.ShapeDtypeStruct(gate_weight.shape, BF),
            jax.ShapeDtypeStruct(up_weight.shape, BF),
            jax.ShapeDtypeStruct(down_weight.shape, BF),
        ),
        in_specs=[pl.BlockSpec(memory_space=pltpu.SMEM)] + [vmem] * 4 + [hbm] * 3,
        out_specs=(hbm,) * 4,
        scratch_shapes=[
            pltpu.VMEM(gate_weight.shape, BF),
            pltpu.VMEM(up_weight.shape, BF),
            pltpu.VMEM(down_weight.shape, BF),
            pltpu.VMEM(tokens.shape, BF),
            pltpu.VMEM(gate_weight.shape, BF),
            pltpu.VMEM(up_weight.shape, BF),
            pltpu.VMEM(down_weight.shape, BF),
            pltpu.SemaphoreType.DMA((10,)),
            pltpu.VMEM((32, 128, 512), BF),
            pltpu.VMEM((32, 128, 512), BF),
            pltpu.VMEM((8, 4, 16, 128), F32),
            pltpu.VMEM((8, 2, 16, 128), F32),
            pltpu.VMEM((8, 4, 16, 128), F32),
            pltpu.VMEM((3, 4, 192, 512), BF),
            pltpu.VMEM((3, 4, 192, 512), BF),
            pltpu.VMEM((3, 32, 128), F32),
            pltpu.VMEM((3, 32, 128), F32),
            pltpu.VMEM((8, 8, 128), F32),
            pltpu.VMEM((4, 192, w), BF),
            pltpu.VMEM((4, 192, w), BF),
            pltpu.VMEM((2, 192, w), F32),
            pltpu.VMEM((4, 3, 48, w), BF),
            pltpu.VMEM((4, 3, 48, w), BF),
            pltpu.VMEM((4, 48, w), BF),
            pltpu.VMEM((4, 48, w), BF),
            pltpu.VMEM((2, 4, 4, 48, w), BF),
            pltpu.VMEM((4, 4, 48, 2 * FF), BF),
            pltpu.VMEM((4, 2, 4, 48, 512), BF),
            pltpu.VMEM((4, 4, 2, 48, 512), BF),
            pltpu.VMEM((8, 128, 512), BF),
            pltpu.VMEM((8, 128, 512), BF),
            pltpu.VMEM((128, 512), F32),
        ]
        + dma(3)
        + dma(8)
        + dma(3)
        + dma(2, 4, 4)
        + dma(2, 4)
        + dma(4, 8)
        + dma(4)
        + dma(4, 3)
        + dma(4)
        + dma(4, 7)
        + dma(4, 7)
        + dma(4, 3)
        + dma(8),
        compiler_params=pltpu.CompilerParams(
            collective_id=0, has_side_effects=True, vmem_limit_bytes=62 << 20
        ),
        cost_estimate=pl.CostEstimate(flops=10_000_000_000, bytes_accessed=10_000_000, transcendentals=0),
        name="expert_layer",
    )(
        swap_plan, tokens, cotangent, expert_ids.T, gate_values.T, gate_weight, up_weight, down_weight
    )
    return pl.pallas_call(
        hand_out,
        out_shape=tuple(jax.ShapeDtypeStruct(o.shape, o.dtype) for o in outs),
        in_specs=[hbm] * 4,
        out_specs=(hbm,) * 4,
        scratch_shapes=[pltpu.VMEM(o.shape, o.dtype) for o in outs] + [pltpu.SemaphoreType.DMA((2, 7))],
        name="hand_out",
    )(*outs)


def solution(mesh):
    return jax.shard_map(
        shards,
        mesh=mesh,
        in_specs=(
            P("dp", "expert"),
            P("dp", "expert"),
            P("dp", None),
            P("dp", None),
            P(),
            P("dp", "expert", None),
            P("dp", "expert", None),
            P("dp", None, "expert"),
        ),
        out_specs=(
            P("dp", "expert"),
            P("dp", "expert", None),
            P("dp", "expert", None),
            P("dp", None, "expert"),
        ),
        check_vma=False,
    )
```

```python
import functools

import jax
import jax.numpy as jnp
from jax import lax
from jax.experimental import pallas as pl
from jax.experimental.pallas import tpu as pltpu
from jax.sharding import PartitionSpec as P

BF = jnp.bfloat16
F32 = jnp.float32
MESH = pl.DeviceIdType.MESH
NX, NZ, NY = 4, 8, 4
FF = 768
PAIRS = ((7, 1), (6, 2), (5, 3), (0, 4))


def dot(a, b):
    return lax.dot_general(a, b, (((1,), (0,)), ((), ())), preferred_element_type=F32)


def dot_nt(a, b):
    return lax.dot_general(a, b, (((1,), (1,)), ((), ())), preferred_element_type=F32)


def dot_tn(a, b):
    return lax.dot_general(a, b, (((0,), (0,)), ((), ())), preferred_element_type=F32)


def kernel(
    plan, tok, cot, ids_in, gates_in, wg_in, wu_in, wd_in,
    tg_out, gg_out, ug_out, dg_out,
    wg, wu, wd, tg_o, gg_o, ug_o, dg_o, near_s,
    T, C, M, M2, MF, X, G, RK, GV, RK2, CS, CR, H, SY, RY, PS, PR, AB, AH, R, RB, DS, ZR, OWN,
    mx_s, mx_r, mz_s, mz_r, ax_s, ax_r, az_s, az_r, bz_s, bz_r, bx_s, bx_r, cs_s, cs_r,
    sy_s, sy_r, ps_s, ps_r, ag_s, ag_r, ah_s, ah_r, rx_s, rx_r, rz_s, rz_r,
):
    dp = lax.axis_index("dp")
    ex = lax.axis_index("expert")
    x, z = lax.div(dp, NZ), lax.rem(dp, NZ)
    y, c = lax.div(ex, 2), lax.rem(ex, 2)
    other = 1 - c

    def at(xx, zz):
        return lax.rem(xx, NX) * NZ + lax.rem(zz, NZ)

    turn = 1 + 2 * c
    y_a, y_b, y_opp = lax.rem(y + turn, NY), lax.rem(y + NY - turn, NY), lax.rem(y + 2, NY)
    peer = (dp, y * 2 + other)
    to_a, to_b = (dp, y_a * 2 + c), (dp, y_b * 2 + c)
    x_to = [None] + [(at(x + j, z), ex) for j in (1, 2, 3)]
    z_to = [None] + [(at(x, z + i), ex) for i in range(1, NZ)]

    moves = [(wg_in, wg), (wu_in, wu), (wd_in, wd)]
    moves += [(gg_o.at[0], gg_out.at[0]), (ug_o.at[0], ug_out.at[0]), (dg_o.at[1], dg_out.at[1])]
    moves += [(gg_o.at[1], gg_out.at[1]), (ug_o.at[1], ug_out.at[1]), (dg_o.at[0], dg_out.at[0])]
    moves += [(tg_o, tg_out)]

    def local(n):
        return pltpu.make_async_copy(moves[n][0], moves[n][1], near_s.at[n])

    for n in range(3):
        local(n).start()

    barrier = pltpu.get_barrier_semaphore()
    group = [peer, to_a, to_b] + x_to[1:] + z_to[1:]
    for device in group:
        pl.semaphore_signal(barrier, inc=1, device_id=device, device_id_type=MESH)
    pl.semaphore_wait(barrier, len(group))

    def rc(src, dst, s, r, to):
        return pltpu.make_async_remote_copy(
            src_ref=src, dst_ref=dst, send_sem=s, recv_sem=r, device_id=to, device_id_type=MESH
        )

    sent = []

    def go(*how):
        copy = rc(*how)
        copy.start()
        sent.append(copy)
        return copy

    mx, mz, ax, az, bz, bx = {}, {}, {}, {}, {}, {}

    def send_az(way, j, h):
        b = at(x + 4 - j, z + (8 - (h - 1) if way == 0 else h - 1))
        az[way, j, h] = go(
            T.at[b] if (j or h > 1) else tok, T.at[b], az_s.at[way, j, h - 1], az_r.at[way, j, h - 1],
            z_to[1] if way == 0 else z_to[7],
        )

    def send_bz(way, h):
        b = at(x, z + (8 - (h - 1) if way == 0 else h - 1))
        bz[way, h] = go(
            C.at[b] if h > 1 else cot, C.at[b], bz_s.at[way, h - 1], bz_r.at[way, h - 1],
            z_to[1] if way == 0 else z_to[7],
        )

    def send_bx(d):
        b = at(x, z + d)
        for n, to in ((0, x_to[1]), (1, x_to[3])):
            bx[n, d] = go(C.at[b] if d else cot, C.at[b], bx_s.at[n, d], bx_r.at[n, d], to)

    def pass_bx(d):
        for n, (off, xx, to) in enumerate(((0, x + 3, x_to[1]), (64, x + 1, x_to[3]))):
            bx[n, d].wait_recv()
            piece = C.at[at(xx, z + d), pl.ds(off, 64)]
            bx[2 + n, d] = go(piece, piece, bx_s.at[2 + n, d], bx_r.at[2 + n, d], to)

    def last(way, j):
        return 4 if (j + way) % 2 == 0 else 3

    M[z, x, 0:8, :] = ids_in[...].astype(F32)
    M[z, x, 8:16, :] = gates_in[...]
    for j in (1, 2, 3):
        mx[j] = go(M.at[z, x], M.at[z, x], mx_s.at[j - 1], mx_r.at[j - 1], x_to[j])
    for j in (1, 2, 3):
        ax[j] = go(tok, T.at[dp], ax_s.at[j - 1], ax_r.at[j - 1], x_to[j])
    send_bz(0, 1)
    send_bz(1, 1)
    send_bx(0)
    for j in (1, 2, 3):
        mx[j].wait_recv()
    for i in range(1, NZ):
        part_m = M.at[z, pl.ds(2 * c, 2)]
        mz[i] = go(part_m, part_m, mz_s.at[i], mz_r.at[i], z_to[i])
    send_az(0, 0, 1)
    send_az(1, 0, 1)
    T[dp] = tok[...]
    C[dp] = cot[...]

    def hop_ax(j):
        ax[j].wait_recv()
        send_az(0, j, 1)
        send_az(1, j, 1)

    def hop_b(h):
        for way in (0, 1):
            if h <= 4 - way:
                bz[way, h].wait_recv()
                if h < 4 - way:
                    send_bz(way, h + 1)
                send_bx(8 - h if way == 0 else h)

    def hop_a(h, *js):
        for j in js:
            for way in (0, 1):
                if h <= last(way, j):
                    az[way, j, h].wait_recv()
                    if h < last(way, j):
                        send_az(way, j, h + 1)

    def places_out():
        for i in range(1, NZ):
            mz[i].wait_recv()
        part_m = M.at[:, pl.ds(2 * c, 2)]
        mz[0] = go(part_m, M2, mz_s.at[0], mz_r.at[0], peer)

    def all_places():
        mz[0].wait_recv()
        MF[:, pl.ds(2 * c, 2)] = M[:, pl.ds(2 * c, 2)]
        MF[:, pl.ds(2 * other, 2)] = M2[...]
        flag = jnp.full((1, 128), plan[dp].astype(F32))
        far = lax.rem(dp + NX * NZ // 2, NX * NZ)
        own_id = (2 * dp + 1).astype(F32)
        star_id = flag * (2 * far + 1).astype(F32) + (1.0 - flag) * own_id
        row_i = lax.broadcasted_iota(jnp.int32, (128, 128), 0)
        col_i = lax.broadcasted_iota(jnp.int32, (128, 128), 1)
        upper = jnp.where(row_i <= col_i, 1.0, 0.0).astype(BF)

        def places(ids, target):
            match = ids == target
            hit = jnp.sum(jnp.where(match, 1.0, 0.0), axis=1)
            return match, jnp.where(hit > 0.0, dot(hit.astype(BF), upper) - 1.0, -1000.0)

        ids = MF[:, :, 0:8, :].reshape(32, 8, 128)
        gates = MF[:, :, 8:16, :].reshape(32, 8, 128)
        for i, target in enumerate(((2 * dp).astype(F32), own_id, star_id[:, None, :])):
            match, rank = places(ids, target)
            RK[i] = rank
            GV[i] = jnp.sum(jnp.where(match, gates, 0.0), axis=1)
        near = MF[:, pl.ds(x, 1), 0:8, :].reshape(8, 8, 128)
        for j in range(4):
            for e in (0, 1):
                _, rank = places(near, (2 * at(x + 4 - j, z) + e).astype(F32))
                RK2[j * 2 + e] = rank

    slot_i = lax.broadcasted_iota(jnp.int32, (48, 256), 0).astype(F32)

    def tiles(body, n=9, width=256):
        def step(i, carry):
            body(pl.ds(pl.multiple_of(i * width, width), width))
            return carry

        lax.fori_loop(0, n, step, 0)

    def pick(ch):
        da, db = PAIRS[ch]
        for d in (da, db):
            for n in (2, 3):
                bx[n, d].wait_recv()

        def step(j, carry):
            ba, bb = at(j, z + da), at(j, z + db)
            ra = lax.rem(z + da, NZ) * 4 + j
            rb = lax.rem(z + db, NZ) * 4 + j
            ones, scale = [], []
            for i in range(3):
                r0 = RK[i, pl.ds(ra, 1), :]
                r1 = RK[i, pl.ds(rb, 1), :] + 24.0
                eq = slot_i == jnp.concatenate([r0, r1], axis=1)
                g = jnp.concatenate([GV[i, pl.ds(ra, 1), :], GV[i, pl.ds(rb, 1), :]], axis=1)
                ones.append(jnp.where(eq, 1.0, 0.0).astype(BF))
                scale.append(jnp.sum(jnp.where(eq, g, 0.0), axis=1, keepdims=True))
            ones = jnp.concatenate(ones, axis=0)
            scale = jnp.concatenate(scale, axis=0)
            xs = dot(ones, jnp.concatenate([T[ba], T[bb]], axis=0)).astype(BF)
            gs = (dot(ones, jnp.concatenate([C[ba], C[bb]], axis=0)) * scale).astype(BF)
            rows = pl.ds(pl.multiple_of(48 * j, 16), 48)
            for i in range(3):
                X[i, ch, rows, :] = xs[48 * i : 48 * i + 48]
                G[i, ch, rows, :] = gs[48 * i : 48 * i + 48]
            return carry

        lax.fori_loop(0, 4, step, 0)

    cs, sy = {}, {}

    def project(ch):
        for own in (False, True):
            e = c if own else other
            for kind, w in enumerate((wg, wu, wd)):
                for n in range(0, FF, 256):
                    if kind < 2:
                        res = dot(X[e, ch], w[e, :, n : n + 256])
                    else:
                        res = dot_nt(G[e, ch], w[e, n : n + 256, :])
                    col = slice(kind * FF + n, kind * FF + n + 256)
                    if own:
                        H[ch % 2, :, col] = res
                    else:
                        CS[ch, :, col] = res.astype(BF)
            if not own:
                cs[ch] = go(CS.at[ch], CR.at[ch], cs_s.at[ch], cs_r.at[ch], peer)

    def part(ch, yy, col):
        rows = pl.ds(pl.multiple_of(yy * 48, 16), 48)
        return H[ch % 2, rows, col] + CR[ch, rows, col].astype(F32)

    def message(ch, m, yy, to, plus=None):
        def body(col):
            v = part(ch, yy, col)
            if plus is not None:
                v = v + RY[ch, plus, :, col].astype(F32)
            SY[ch, m, :, col] = v.astype(BF)

        tiles(body)
        sy[ch, m] = go(SY.at[ch, m], RY.at[ch, m], sy_s.at[ch, m], sy_r.at[ch, m], to)

    def ring_one(ch):
        cs[ch].wait_recv()
        message(ch, 0, y_opp, to_a)
        message(ch, 1, y_b, to_b)

    def ring_two(ch):
        sy[ch, 0].wait_recv()
        message(ch, 2, y_a, to_a, plus=0)

    swaps = lambda ch: rc(PS.at[ch], PR.at[ch], ps_s.at[ch], ps_r.at[ch], x_to[2])

    def activate(ch):
        sy[ch, 1].wait_recv()
        sy[ch, 2].wait_recv()

        def body(i, carry):
            cols = [pl.ds(pl.multiple_of(k * FF + i * 128, 128), 128) for k in range(3)]

            def total(col):
                v = part(ch, y, col)
                return v + RY[ch, 1, :, col].astype(F32) + RY[ch, 2, :, col].astype(F32)

            gate, up, back = [total(col) for col in cols]
            sig = jax.nn.sigmoid(gate)
            silu = gate * sig
            PS[ch, :, cols[0]] = (silu * up).astype(BF)
            PS[ch, :, cols[1]] = (back * up * sig * (1.0 + gate * (1.0 - sig))).astype(BF)
            PS[ch, :, cols[2]] = (back * silu).astype(BF)
            return carry

        lax.fori_loop(0, 6, body, 0)

        @pl.when(c == 1)
        def _():
            swaps(ch).start()
            AH[ch, y] = PS[ch, :, FF:]
            for n, to in ((0, to_a), (1, to_b), (2, peer)):
                ah(ch, n, y, to).start()

        @pl.when(c == 0)
        def _():
            AB[0, ch, y] = PS[ch]
            for n, to in ((0, to_a), (1, to_b), (2, peer)):
                ag(ch, n, y, to).start()

    def ag(ch, n, yy, to):
        block = AB.at[c, ch, yy]
        return rc(block, block, ag_s.at[ch, n], ag_r.at[ch, n], to)

    def ah(ch, n, yy, to):
        block = AH.at[ch, yy]
        return rc(block, block, ah_s.at[ch, n], ah_r.at[ch, n], to)

    def choose(ch):
        @pl.when(c == 1)
        def _():
            swaps(ch).wait_recv()

            def body(col):
                keep = jnp.full((48, 256), plan[dp].astype(F32)) > 0.5
                v = jnp.where(keep, PR[ch, :, col].astype(F32), PS[ch, :, col].astype(F32))
                AB[1, ch, y, :, col] = v.astype(BF)

            tiles(body)
            for n, to in ((0, to_a), (1, to_b), (2, peer)):
                ag(ch, n, y, to).start()

    def pass_on(block, ch):
        block(ch, 0, y_b, to_a).wait_recv()
        block(ch, 3, y_b, to_a).start()
        block(ch, 4, y_b, peer).start()
        block(ch, 1, y_a, to_b).wait_recv()
        block(ch, 5, y_a, peer).start()

    def pass_end(block, ch):
        block(ch, 3, y_opp, to_a).wait_recv()
        block(ch, 6, y_opp, peer).start()

    def on_cores(zero, one):
        if zero is not None:
            pl.when(c == 0)(zero)
        pl.when(c == 1)(one)

    def tok_pass(ch):
        on_cores(lambda: pass_on(ag, ch), lambda: pass_on(ah, ch))

    def tok_end(ch):
        on_cores(lambda: pass_end(ag, ch), lambda: pass_end(ah, ch))

    def peer_in(block, ch):
        for n in (2, 4, 5, 6):
            block(ch, n, y, peer).wait_recv()

    def tok_done(ch):
        on_cores(lambda: peer_in(ah, ch), lambda: peer_in(ag, ch))

    def star_pass(ch):
        on_cores(None, lambda: pass_on(ag, ch))

    def star_end(ch):
        on_cores(None, lambda: pass_end(ag, ch))

    def star_done(ch):
        pl.when(c == 0)(lambda: peer_in(ag, ch))

    rx = {}

    def rows_of(ch, e):
        gd = (AB[0, ch, :, :, FF : 2 * FF] if e == 0 else AH[ch, :, :, :FF]).reshape(192, FF)
        ud = (AB[0, ch, :, :, 2 * FF :] if e == 0 else AH[ch, :, :, FF:]).reshape(192, FF)
        for n in (0, 256):
            res = dot_nt(gd, wg[e, n : n + 256, :]) + dot_nt(ud, wu[e, n : n + 256, :])
            R[ch, e, :, :, n : n + 256] = res.astype(BF).reshape(4, 48, 256)

    def send_rows(ch, k, e):
        for j in (1, 2, 3):
            rx[ch, k, j] = go(
                R.at[ch, e, lax.rem(x + j, NX)], RB.at[ch, j, e], rx_s.at[ch, k, j - 1],
                rx_r.at[ch, k, j - 1], x_to[j],
            )

    def back_rows(ch):
        on_cores(lambda: rows_of(ch, 0), lambda: rows_of(ch, 1))
        send_rows(ch, 0, c)
        tok_done(ch)
        on_cores(lambda: rows_of(ch, 1), lambda: rows_of(ch, 0))
        send_rows(ch, 1, other)

    rz = {}

    def spread(ch):
        for j in (1, 2, 3):
            rx[ch, 0, j].wait_recv()
            rx[ch, 1, j].wait_recv()
        da, db = PAIRS[ch]
        za, zb = lax.rem(z + da, NZ), lax.rem(z + db, NZ)
        pieces = []
        for s in range(8):
            r0 = RK2[s, pl.ds(za, 1), :]
            r1 = RK2[s, pl.ds(zb, 1), :] + 24.0
            pieces.append(jnp.where(slot_i == jnp.concatenate([r0, r1], axis=1), 1.0, 0.0).astype(BF))
        own = dot_tn(jnp.concatenate(pieces[:2], axis=0), R[ch, :, pl.ds(x, 1)].reshape(96, 512))
        rest = dot_tn(jnp.concatenate(pieces[2:], axis=0), RB[ch, 1:].reshape(288, 512))
        v = own + rest
        for i, d in ((1, db), (0, da)):
            block = v[128 * i : 128 * i + 128]
            if d == 0:
                OWN[...] = block
            else:
                DS[d] = block.astype(BF)
                rz[d] = go(DS.at[d], ZR.at[d], rz_s.at[d], rz_r.at[d], z_to[d])

    def input_grads(slot, i):
        def inputs(n, carry):
            d = pl.ds(pl.multiple_of(n * 256, 256), 256)
            xs = X[i, :, :, d].reshape(FF, 256)
            for k, out in ((1, gg_o), (2, ug_o)):
                act = AB[slot, :, :, :, k * FF : (k + 1) * FF].reshape(FF, FF)
                out[slot, d, :] = dot_tn(xs, act).astype(BF)
            return carry

        lax.fori_loop(0, 2, inputs, 0)

    def hidden_grads(slot, i):
        def hidden(n, carry):
            f = pl.ds(pl.multiple_of(n * 256, 256), 256)
            hid = AB[slot, :, :, :, f].reshape(FF, 256)
            dg_o[slot, f, :] = dot_tn(hid, G[i].reshape(FF, 512)).astype(BF)
            return carry

        lax.fori_loop(0, 3, hidden, 0)

    def forward(ch):
        pick(ch)
        project(ch)

    hop_ax(1)
    hop_ax(3)
    hop_b(1)
    hop_ax(2)
    pass_bx(0)
    hop_a(1, 0)
    hop_b(2)
    hop_a(1, 1)
    places_out()
    pass_bx(7)
    pass_bx(1)
    hop_a(1, 3)
    hop_b(3)
    for n in range(3):
        local(n).wait()
    all_places()
    hop_a(1, 2)
    forward(0)
    pass_bx(6)
    pass_bx(2)
    hop_a(2, 0, 1)
    hop_b(4)
    ring_one(0)
    hop_a(2, 3, 2)
    pass_bx(5)
    pass_bx(3)
    ring_two(0)
    forward(1)
    pass_bx(4)
    activate(0)
    ring_one(1)
    tok_pass(0)
    ring_two(1)
    hop_a(3, 0, 1, 3, 2)
    forward(2)
    tok_end(0)
    activate(1)
    ring_one(2)
    choose(0)
    back_rows(0)
    tok_pass(1)
    ring_two(2)
    hop_a(4, 0, 1, 3, 2)
    forward(3)
    tok_end(1)
    activate(2)
    ring_one(3)
    star_pass(0)
    choose(1)
    back_rows(1)
    spread(0)
    tok_pass(2)
    ring_two(3)
    tok_end(2)
    star_end(0)
    activate(3)
    star_pass(1)
    choose(2)
    back_rows(2)
    spread(1)
    tok_pass(3)
    star_end(1)
    choose(3)
    tok_end(3)
    star_pass(2)
    spread(2)
    back_rows(3)
    star_end(2)
    star_pass(3)
    hidden_grads(0, 0)
    local(8).start()
    spread(3)
    star_end(3)
    input_grads(0, 0)
    local(3).start()
    local(4).start()
    for ch in range(4):
        star_done(ch)
    hidden_grads(1, 2)
    local(5).start()
    input_grads(1, 2)
    local(6).start()
    local(7).start()

    total = OWN[...]
    for d in (1, 7, 2, 6, 3, 5, 4):
        rz[d].wait_recv()
        total = total + ZR[d].astype(F32)
    tg_o[...] = total.astype(BF)
    local(9).start()
    for n in range(3, 10):
        local(n).wait()
    for copy in sent:
        copy.wait_send()
    for ch in range(4):
        for n in range(7):
            ag(ch, n, y, peer).wait_send()

        @pl.when(c == 1)
        def _():
            swaps(ch).wait_send()
            for n in range(7):
                ah(ch, n, y, peer).wait_send()


def hand_out(tg, gg, ug, dg, tg_o, gg_o, ug_o, dg_o, tg_v, gg_v, ug_v, dg_v, sem):
    steps = [(tg, tg_v, tg_o)]
    for src, mid, dst in ((gg, gg_v, gg_o), (ug, ug_v, ug_o), (dg, dg_v, dg_o)):
        steps += [(src.at[e], mid.at[e], dst.at[e]) for e in (0, 1)]
    first = [pltpu.make_async_copy(a, b, sem.at[0, n]) for n, (a, b, _) in enumerate(steps)]
    then = [pltpu.make_async_copy(b, d, sem.at[1, n]) for n, (_, b, d) in enumerate(steps)]
    for copy in first:
        copy.start()
    for one, two in zip(first, then):
        one.wait()
        two.start()
    for copy in then:
        copy.wait()


def shards(tokens, cotangent, expert_ids, gate_values, swap_plan, gate_weight, up_weight, down_weight):
    vmem = pl.BlockSpec(memory_space=pltpu.VMEM)
    hbm = pl.BlockSpec(memory_space=pl.ANY)
    dma = lambda *shape: [pltpu.SemaphoreType.DMA(shape), pltpu.SemaphoreType.DMA(shape)]
    w = 3 * FF
    outs = pl.pallas_call(
        kernel,
        out_shape=(
            jax.ShapeDtypeStruct(tokens.shape, BF),
            jax.ShapeDtypeStruct(gate_weight.shape, BF),
            jax.ShapeDtypeStruct(up_weight.shape, BF),
            jax.ShapeDtypeStruct(down_weight.shape, BF),
        ),
        in_specs=[pl.BlockSpec(memory_space=pltpu.SMEM)] + [vmem] * 4 + [hbm] * 3,
        out_specs=(hbm,) * 4,
        scratch_shapes=[
            pltpu.VMEM(gate_weight.shape, BF),
            pltpu.VMEM(up_weight.shape, BF),
            pltpu.VMEM(down_weight.shape, BF),
            pltpu.VMEM(tokens.shape, BF),
            pltpu.VMEM(gate_weight.shape, BF),
            pltpu.VMEM(up_weight.shape, BF),
            pltpu.VMEM(down_weight.shape, BF),
            pltpu.SemaphoreType.DMA((10,)),
            pltpu.VMEM((32, 128, 512), BF),
            pltpu.VMEM((32, 128, 512), BF),
            pltpu.VMEM((8, 4, 16, 128), F32),
            pltpu.VMEM((8, 2, 16, 128), F32),
            pltpu.VMEM((8, 4, 16, 128), F32),
            pltpu.VMEM((3, 4, 192, 512), BF),
            pltpu.VMEM((3, 4, 192, 512), BF),
            pltpu.VMEM((3, 32, 128), F32),
            pltpu.VMEM((3, 32, 128), F32),
            pltpu.VMEM((8, 8, 128), F32),
            pltpu.VMEM((4, 192, w), BF),
            pltpu.VMEM((4, 192, w), BF),
            pltpu.VMEM((2, 192, w), F32),
            pltpu.VMEM((4, 3, 48, w), BF),
            pltpu.VMEM((4, 3, 48, w), BF),
            pltpu.VMEM((4, 48, w), BF),
            pltpu.VMEM((4, 48, w), BF),
            pltpu.VMEM((2, 4, 4, 48, w), BF),
            pltpu.VMEM((4, 4, 48, 2 * FF), BF),
            pltpu.VMEM((4, 2, 4, 48, 512), BF),
            pltpu.VMEM((4, 4, 2, 48, 512), BF),
            pltpu.VMEM((8, 128, 512), BF),
            pltpu.VMEM((8, 128, 512), BF),
            pltpu.VMEM((128, 512), F32),
        ]
        + dma(3)
        + dma(8)
        + dma(3)
        + dma(2, 4, 4)
        + dma(2, 4)
        + dma(4, 8)
        + dma(4)
        + dma(4, 3)
        + dma(4)
        + dma(4, 7)
        + dma(4, 7)
        + dma(4, 2, 3)
        + dma(8),
        compiler_params=pltpu.CompilerParams(
            collective_id=0, has_side_effects=True, vmem_limit_bytes=62 << 20
        ),
        cost_estimate=pl.CostEstimate(flops=10_000_000_000, bytes_accessed=10_000_000, transcendentals=0),
        name="expert_layer",
    )(
        swap_plan, tokens, cotangent, expert_ids.T, gate_values.T, gate_weight, up_weight, down_weight
    )
    return pl.pallas_call(
        hand_out,
        out_shape=tuple(jax.ShapeDtypeStruct(o.shape, o.dtype) for o in outs),
        in_specs=[hbm] * 4,
        out_specs=(hbm,) * 4,
        scratch_shapes=[pltpu.VMEM(o.shape, o.dtype) for o in outs] + [pltpu.SemaphoreType.DMA((2, 7))],
        name="hand_out",
    )(*outs)


def solution(mesh):
    return jax.shard_map(
        shards,
        mesh=mesh,
        in_specs=(
            P("dp", "expert"),
            P("dp", "expert"),
            P("dp", None),
            P("dp", None),
            P(),
            P("dp", "expert", None),
            P("dp", "expert", None),
            P("dp", None, "expert"),
        ),
        out_specs=(
            P("dp", "expert"),
            P("dp", "expert", None),
            P("dp", "expert", None),
            P("dp", None, "expert"),
        ),
        check_vma=False,
    )
```
